128 devices in a mesh: ctx: 32 (over z, x, core), kvh: 4 (over y).
Axes of the slice: x: 4, y: 4, z: 4, core: 2. Of those that a mesh axis runs over, the one named last changes fastest.
Arguments:
- queries: bfloat16 [256, 16384], P('ctx', 'kvh'), may hold values from -96 to 96
- cache: bfloat16 [8, 65536, 8, 256], P(None, 'ctx', 'kvh'), may hold values from -6 to 6, as said below
- new_kv: bfloat16 [8, 32, 8, 256], P(None, None, 'kvh'), may hold values from -6 to 6
- lengths: int32 [8], replicated, may hold values from 26625 to 65536, as said below
- out_weight: bfloat16 [16384, 16384], P('kvh', 'ctx'), may hold values from -3 to 3
Outputs:
- projected: bfloat16 [256, 16384], P('kvh', 'ctx')
The draws below stay inside these ranges and needn't reach their ends.
Inputs may be any that keep to these rules, and one draw needn't show every extreme that they name: `lengths`: the longest request's length equals 65536. `cache`: entries at positions at or beyond a request's length are never read.
All inputs are finite; a program needn't handle non-finite values.
Results may differ from the reference program's by a relative error of at most 0.0063.
Values may be sent and summed in bfloat16 or wider, within the bound.
No kernel may reach another device: no remote copies, remote signals or barrier semaphores. Data moves between devices by JAX's collectives and lax.ppermute only.
A program may use at most 320 MiB of HBM per device.

```python
import jax
import jax.numpy as jnp
from jax import lax

D = 16384
QH = 128
KV_HEADS = 8
HD = 128
REQS = 8
NEW = 32
SLOT = 2048
CAP = 65536
N_CTX = 32


def draw_cache(key, part):
    key = jax.random.fold_in(key, 1)
    base = jnp.clip(jax.random.normal(key, (REQS, CAP, KV_HEADS, 2 * HD), jnp.float32), -6.0, 6.0)
    return base.astype(jnp.bfloat16)


def draw_queries(key, part):
    key = jax.random.fold_in(key, 2)
    base = jnp.clip(jax.random.normal(key, (REQS * NEW, QH, HD), jnp.float32), -6.0, 6.0)
    return base.reshape(REQS * NEW, QH * HD).astype(jnp.bfloat16)


def draw_lengths(key, part):
    key = jax.random.fold_in(key, 3)
    first, second = jax.random.split(key)
    table = jnp.array([7, 8, 9, 10, 11, 13, 14, 16], jnp.int32)
    fracs = table[jax.random.permutation(first, 8)]
    base = fracs * (CAP // 16)
    jitter = jax.random.randint(second, (REQS,), 0, CAP // 32)
    return jnp.where(fracs == 16, base, base - jitter).astype(jnp.int32)


def levels(own_key, shape, shards, least, high):
    def one(dim, blocks):
        draws = jax.random.uniform(jax.random.fold_in(jax.random.fold_in(own_key, 6), dim), (blocks,), jnp.float32, least / len(shards), high / len(shards))
        return jnp.repeat(jnp.exp(draws), shape[dim] // blocks).reshape((-1,) + (1,) * (len(shape) - dim - 1))

    loudness = one(*shards[0])
    for cut in shards[1:]:
        loudness = loudness * one(*cut)
    return loudness


def noise(stream_key, dims, width, bound, shards=(), held_as=jnp.bfloat16):
    values = width * jax.random.normal(stream_key, dims, jnp.float32)
    if shards:
        values = values * levels(stream_key, dims, shards, -0.22, 0.18)
    return jnp.clip(values, -bound, bound).astype(held_as)


def setup_inputs(seed: int = 0) -> dict:
    key_list = jax.random.split(jax.random.key(seed), 6)
    queries = draw_queries(jax.random.fold_in(key_list[5], 71), 0)
    cache = draw_cache(jax.random.fold_in(key_list[5], 71), 0)
    new_kv = noise(key_list[2], (REQS, NEW, KV_HEADS, 2 * HD), 1.0, 6.0, ((2, 4),))
    lengths = draw_lengths(jax.random.fold_in(key_list[5], 71), 0)
    out_weight = noise(key_list[4], (D, D), 0.5, 3.0, ((0, 4), (1, 32)))
    return dict(queries=queries, cache=cache, new_kv=new_kv, lengths=lengths, out_weight=out_weight)


def partial_scores(qblock, keys, values, valid):
    scores = jnp.dot(qblock, keys.T, preferred_element_type=jnp.float32) * (HD ** -0.5)
    scores = jnp.where(valid, scores, -1e30)
    top = jnp.max(scores, axis=1)
    weights = jnp.where(valid, jnp.exp(scores - top[:, None]), 0.0)
    total = jnp.sum(weights, axis=1)
    summed = jnp.dot(weights.astype(jnp.bfloat16), values, preferred_element_type=jnp.float32)
    return top, total, summed


def reference(queries, cache, new_kv, lengths, out_weight):
    group = QH // KV_HEADS
    grouped = queries.reshape(REQS, NEW, KV_HEADS, group * HD)
    positions = jnp.arange(CAP, dtype=jnp.int32).reshape(N_CTX, SLOT)

    def one(pair):
        req = pair // KV_HEADS
        head = pair % KV_HEADS
        qblock = grouped[req, :, head].reshape(NEW * group, HD)
        keys = cache[req, :, head, :HD].reshape(N_CTX, SLOT, HD)
        values = cache[req, :, head, HD:].reshape(N_CTX, SLOT, HD)

        def shard(index):
            valid = (positions[index] < lengths[req])[None, :]
            top, total, summed = partial_scores(qblock, keys[index], values[index], valid)
            normal = (summed / jnp.maximum(total, 1.0)[:, None]).astype(jnp.bfloat16)
            return top, total, normal

        tops, totals, normals = lax.map(shard, jnp.arange(N_CTX, dtype=jnp.int32))
        sums = totals[..., None] * normals.astype(jnp.float32)
        token = jnp.arange(NEW * group, dtype=jnp.int32) // group
        valid_new = jnp.arange(NEW, dtype=jnp.int32)[None, :] <= token[:, None]
        top_n, total_n, sum_n = partial_scores(qblock, new_kv[req, :, head, :HD], new_kv[req, :, head, HD:], valid_new)
        tops = jnp.concatenate([tops, top_n[None]], axis=0)
        totals = jnp.concatenate([totals, total_n[None]], axis=0)
        sums = jnp.concatenate([sums, sum_n[None]], axis=0)
        best = jnp.max(tops, axis=0)
        factor = jnp.exp(tops - best[None])
        total = jnp.sum(factor * totals, axis=0)
        summed = jnp.sum(factor[:, :, None] * sums, axis=0)
        return (summed / total[:, None]).astype(jnp.bfloat16).reshape(NEW, group * HD)

    attended = lax.map(one, jnp.arange(REQS * KV_HEADS, dtype=jnp.int32))
    attended = attended.reshape(REQS, KV_HEADS, NEW, group * HD).transpose(0, 2, 1, 3).reshape(REQS * NEW, D)
    return jnp.dot(attended, out_weight, preferred_element_type=jnp.float32).astype(jnp.bfloat16)
```

```python
import functools
import math

import jax
import jax.numpy as jnp
from jax import lax
from jax.experimental import pallas as pl
from jax.experimental.pallas import tpu as pltpu
from jax.sharding import PartitionSpec as P

KV_HEADS = 8
QH = 128
HD = 128
REQS = 8
NEW = 32
GROUP = QH // KV_HEADS
SIDE = 4
ROWS = 16
BLOCK = GROUP * ROWS
FEATS = GROUP * HD
WIDE = FEATS + HD
SCALE = HD ** (-0.5) * math.log2(math.e)
EMPTY = -1e30
F32, BF16 = jnp.float32, jnp.bfloat16
MIB = 2**20


def at(z, x, core):
    return ((z % SIDE) * SIDE + x % SIDE) * 2 + core


def places():
    return [(z, x, c) for z in range(SIDE) for x in range(SIDE) for c in range(2)]


def from_first(value, step):
    pairs = [(at(z, x + step, c) if c == 0 else at(z + step, x, c), at(z, x, c)) for z, x, c in places()]
    return lax.ppermute(value, "ctx", pairs)


def from_second(value, step):
    pairs = [(at(z + step, x, c) if c == 0 else at(z, x + step, c), at(z, x, c)) for z, x, c in places()]
    return lax.ppermute(value, "ctx", pairs)


def from_twin(value):
    return lax.ppermute(value, "ctx", [(at(z, x, 1 - c), at(z, x, c)) for z, x, c in places()])


def from_plane(value, step):
    return lax.ppermute(value, "kvh", [((s + step) % SIDE, s) for s in range(SIDE)])


def dot_nt(a, b):
    return lax.dot_general(a, b, (((1,), (1,)), ((), ())), preferred_element_type=F32)


def weigh(s):
    top = (jnp.max(s, axis=1, keepdims=True) * SCALE).astype(BF16).astype(F32)
    w = jnp.exp2(s * SCALE - top)
    return top, jnp.sum(w, axis=1, keepdims=True), w.astype(BF16)


def put_partial(out, index, top, total, summed):
    lane = lax.broadcasted_iota(jnp.int32, (ROWS, HD), 1)
    high = total.astype(BF16).astype(F32)
    low = total - high
    stats = jnp.zeros((ROWS, HD), F32)
    for g in range(GROUP):
        rows = slice(g * ROWS, (g + 1) * ROWS)
        out[index, :, g * HD : (g + 1) * HD] = summed[rows].astype(BF16)
        stats = jnp.where(lane == g, top[rows], stats)
        stats = jnp.where(lane == GROUP + g, high[rows], stats)
        stats = jnp.where(lane == 2 * GROUP + g, low[rows], stats)
    out[index, :, FEATS:] = stats.astype(BF16)


def assemble(info, own, other, held):
    z, x, core = info[0], info[1], info[2]
    for dz in range(SIDE):
        for dx in range(SIDE):
            chip = ((z + dz) % SIDE) * SIDE + (x + dx) % SIDE

            def place(zero, one, chip=chip):
                zero, one = zero.astype(F32), one.astype(F32)
                for g in range(GROUP):
                    cols = slice(g * HD, (g + 1) * HD)
                    pair = jnp.concatenate([zero[:, cols], one[:, cols]], axis=0)
                    held[chip, g * ROWS : (g + 1) * ROWS, :] = pair.astype(BF16)

            @pl.when(core == 0)
            def _():
                place(own[dz][dx], other[dx][dz])

            @pl.when(core == 1)
            def _():
                place(other[dz][dx], own[dx][dz])


def attend_kernel(with_new, info, valid, *refs):
    own, other, cache = refs[:SIDE], refs[SIDE : 2 * SIDE], refs[2 * SIDE]
    refs = refs[2 * SIDE + 1 :]
    if with_new:
        new, out, new_out, held = refs
    else:
        out, held = refs
    step = pl.program_id(0)

    @pl.when(step == 0)
    def _():
        assemble(info, own, other, held)

    first, second = valid[2 * step], valid[2 * step + 1]
    slot = cache.shape[2]
    full = jnp.logical_and(first == slot, second == slot)
    where = [(r, half) for r in range(2) for half in range(2)]

    def scores(r, half):
        return dot_nt(held[step * SIDE + 2 * r + half], cache[0, r, :, :HD])

    def finish(r, half, s):
        top, total, w = weigh(s)
        summed = jnp.dot(w, cache[0, r, :, HD:], preferred_element_type=F32)
        put_partial(out, 2 * r + half, top, total, summed)

    @pl.when(full)
    def _():
        s = scores(*where[0])
        for i, (r, half) in enumerate(where):
            later = scores(*where[i + 1]) if i + 1 < len(where) else None
            finish(r, half, s)
            s = later

    @pl.when(jnp.logical_not(full))
    def _():
        for r, count in ((0, first), (1, second)):

            @pl.when(count > 0)
            def _(r=r, count=count):
                for half in range(2):
                    s = scores(r, half)
                    position = lax.broadcasted_iota(jnp.int32, s.shape, 1)
                    finish(r, half, jnp.where(position < count, s, EMPTY))

            @pl.when(count <= 0)
            def _(r=r):
                lane = lax.broadcasted_iota(jnp.int32, (ROWS, WIDE), 1)
                tops = jnp.logical_and(lane >= FEATS, lane < FEATS + GROUP)
                none = jnp.where(tops, EMPTY, 0.0).astype(BF16)
                for half in range(2):
                    out[2 * r + half] = none

    if with_new:
        @pl.when(step == pl.num_programs(0) - 1)
        def _():
            z, x = info[0], info[1]
            s = dot_nt(held[z * SIDE + x], new[0, :, :HD])
            token = (x % 2) * ROWS + lax.broadcasted_iota(jnp.int32, s.shape, 0) % ROWS
            key = lax.broadcasted_iota(jnp.int32, s.shape, 1)
            top, total, w = weigh(jnp.where(key <= token, s, EMPTY))
            summed = jnp.dot(w, new[0, :, HD:], preferred_element_type=F32)
            put_partial(new_out, 0, top, total, summed)


def attend(info, valid, own, other, cache, new, head_of):
    per = cache.shape[2]
    queries = pl.BlockSpec((SIDE, ROWS // 2, FEATS), lambda i, info, valid: (0, 0, head_of(info[2])))
    in_specs = [queries] * (2 * SIDE) + [
        pl.BlockSpec((1, 2, per, 2 * HD), lambda i, info, valid: (head_of(info[2]), i, 0, 0))
    ]
    out_specs = [pl.BlockSpec((SIDE, ROWS, WIDE), lambda i, info, valid: (i, 0, 0))]
    out_shape = [jax.ShapeDtypeStruct((SIDE * SIDE, ROWS, WIDE), BF16)]
    args = [*own, *other, cache]
    if new is not None:
        in_specs.append(pl.BlockSpec((1, NEW, 2 * HD), lambda i, info, valid: (0, 0, 0)))
        out_specs.append(pl.BlockSpec((1, ROWS, WIDE), lambda i, info, valid: (0, 0, 0)))
        out_shape.append(jax.ShapeDtypeStruct((1, ROWS, WIDE), BF16))
        args.append(new)
    return pl.pallas_call(
        functools.partial(attend_kernel, new is not None),
        out_shape=out_shape,
        grid_spec=pltpu.PrefetchScalarGridSpec(
            num_scalar_prefetch=2,
            grid=(REQS // 2,),
            in_specs=in_specs,
            out_specs=out_specs,
            scratch_shapes=[pltpu.VMEM((SIDE * SIDE, BLOCK, HD), BF16)],
        ),
        compiler_params=pltpu.CompilerParams(vmem_limit_bytes=48 * MIB),
        cost_estimate=pl.CostEstimate(
            flops=4 * REQS * 2 * BLOCK * per * HD, bytes_accessed=REQS * per * 2 * HD * 2, transcendentals=0
        ),
        name="attend_new" if new is not None else "attend",
    )(info, valid, *args)


def merge(parts):
    parts = [p.astype(F32) for p in parts]
    tops = [p[:, FEATS : FEATS + GROUP] for p in parts]
    totals = [p[:, FEATS + GROUP : FEATS + 2 * GROUP] + p[:, FEATS + 2 * GROUP : FEATS + 3 * GROUP] for p in parts]
    best = functools.reduce(jnp.maximum, tops)
    factors = [jnp.exp2(t - best) for t in tops]
    total = sum(f * t for f, t in zip(factors, totals))
    summed = [
        sum(f[:, g : g + 1] * p[:, g * HD : (g + 1) * HD] for f, p in zip(factors, parts)) for g in range(GROUP)
    ]
    return best, total, summed


def put_merged(out, index, parts):
    best, total, summed = merge(parts)
    high = total.astype(BF16)
    low = (total - high.astype(F32)).astype(BF16)
    for g in range(GROUP):
        out[index, :, g * HD : (g + 1) * HD] = summed[g].astype(BF16)
    rest = jnp.zeros((ROWS, HD - 3 * GROUP), BF16)
    out[index, :, FEATS:] = jnp.concatenate([best.astype(BF16), high, low, rest], axis=1)


def twin_kernel(info, mine, got, new, *outs):
    z, x, core = info[0], info[1], info[2]
    for d in range(SIDE):
        for j in range(SIDE):
            chip = jnp.where(core == 0, ((z + d) % SIDE) * SIDE + j, j * SIDE + (x + d) % SIDE)
            if d == 0:
                own = chip == z * SIDE + x

                @pl.when(own)
                def _():
                    put_merged(outs[d], j, [mine[chip], got[chip], new[0]])

                @pl.when(jnp.logical_not(own))
                def _():
                    put_merged(outs[d], j, [mine[chip], got[chip]])
            else:
                put_merged(outs[d], j, [mine[chip], got[chip]])


def whole():
    return pl.BlockSpec(memory_space=pltpu.VMEM)


def merge_twins(info, mine, got, new):
    return pl.pallas_call(
        twin_kernel,
        out_shape=[jax.ShapeDtypeStruct((SIDE, ROWS, WIDE), BF16)] * SIDE,
        in_specs=[pl.BlockSpec(memory_space=pltpu.SMEM)] + [whole()] * 3,
        out_specs=[whole()] * SIDE,
        compiler_params=pltpu.CompilerParams(vmem_limit_bytes=24 * MIB),
        name="merge_twins",
    )(info, mine, got, new)


def four_kernel(a, b, c, d, out):
    @pl.loop(0, SIDE)
    def _(j):
        put_merged(out, j, [a[j], b[j], c[j], d[j]])


def merge_four(parts):
    return pl.pallas_call(
        four_kernel,
        out_shape=jax.ShapeDtypeStruct((SIDE, ROWS, WIDE), BF16),
        in_specs=[whole()] * SIDE,
        out_specs=whole(),
        compiler_params=pltpu.CompilerParams(vmem_limit_bytes=24 * MIB),
        name="merge_four",
    )(*parts)


def final_kernel(a, b, c, d, out):
    @pl.loop(0, SIDE)
    def _(j):
        _, total, summed = merge([a[j], b[j], c[j], d[j]])
        for g in range(GROUP):
            out[j, :, g * HD : (g + 1) * HD] = (summed[g] / total[:, g : g + 1]).astype(BF16)


def merge_final(parts):
    return pl.pallas_call(
        final_kernel,
        out_shape=jax.ShapeDtypeStruct((SIDE, ROWS, FEATS), BF16),
        in_specs=[whole()] * SIDE,
        out_specs=whole(),
        compiler_params=pltpu.CompilerParams(vmem_limit_bytes=24 * MIB),
        name="merge_final",
    )(*parts)


def project_kernel(info, *refs):
    own, other, weight = refs[:SIDE], refs[SIDE : 2 * SIDE], refs[2 * SIDE]
    keep, sends, held, acc = refs[2 * SIDE + 1], refs[2 * SIDE + 2 : 3 * SIDE + 1], refs[-2], refs[-1]
    step = pl.program_id(0)
    z, x, core, y = info[0], info[1], info[2], info[3]
    depth = weight.shape[0]
    per = FEATS // depth

    @pl.when(step == 0)
    def _():
        acc[...] = jnp.zeros_like(acc)

        def place(zero, one):
            for d in range(SIDE):
                for j in range(SIDE):
                    for half, values, chip in (
                        (0, zero, ((z + d) % SIDE) * SIDE + j),
                        (1, one, j * SIDE + (x + d) % SIDE),
                    ):
                        rows = pl.ds(pl.multiple_of(chip * ROWS, ROWS), ROWS)
                        for k in range(per):
                            held[half * per + k, rows, :] = values[d][j, :, k * depth : (k + 1) * depth]

        @pl.when(core == 0)
        def _():
            place(own, other)

        @pl.when(core == 1)
        def _():
            place(other, own)

    acc[...] += jnp.dot(held[step], weight[...], preferred_element_type=F32)

    @pl.when(step == pl.num_programs(0) - 1)
    def _():
        count = keep.shape[0]
        for d in range(SIDE):
            rows = acc[pl.ds(pl.multiple_of(((y + d) % SIDE) * count, count), count), :]
            if d == 0:
                keep[...] = rows
            else:
                sends[d - 1][...] = rows.astype(BF16)


def project(info, own, other, weight):
    depth = 1024
    cols = weight.shape[1]
    rows = SIDE * SIDE * ROWS
    return pl.pallas_call(
        project_kernel,
        out_shape=[jax.ShapeDtypeStruct((rows // SIDE, cols), F32)]
        + [jax.ShapeDtypeStruct((rows // SIDE, cols), BF16)] * (SIDE - 1),
        grid=(weight.shape[0] // depth,),
        in_specs=[pl.BlockSpec(memory_space=pltpu.SMEM)]
        + [whole()] * (2 * SIDE)
        + [pl.BlockSpec((depth, cols), lambda i: (i, 0))],
        out_specs=[whole()] * SIDE,
        scratch_shapes=[
            pltpu.VMEM((weight.shape[0] // depth, rows, depth), BF16),
            pltpu.VMEM((rows, cols), F32),
        ],
        compiler_params=pltpu.CompilerParams(vmem_limit_bytes=32 * MIB),
        name="project",
    )(info, *own, *other, weight)


def on_device(queries, cache, new_kv, lengths, out_weight):
    index = lax.axis_index("ctx")
    z, x, core = index // (2 * SIDE), (index // 2) % SIDE, index % 2
    info = jnp.stack([z, x, core, lax.axis_index("kvh")]).astype(jnp.int32)
    slot = cache.shape[1]
    valid = jnp.clip(lengths - index * slot, 0, slot).astype(jnp.int32)
    by_head = jnp.transpose(cache, (2, 0, 1, 3))

    line = jnp.stack([queries] + [from_first(queries, s) for s in (1, 2, 3)])
    own = [line] + [from_second(line, s) for s in (1, 2, 3)]
    other = [from_twin(part) for part in own]

    request = 2 * z + x // 2
    new = lax.dynamic_slice(new_kv, (request, 0, core, 0), (1, NEW, 1, 2 * HD)).reshape(1, NEW, 2 * HD)

    (sent,) = attend(info, valid, own, other, by_head, None, lambda c: 1 - c)
    got = from_twin(sent)
    mine, from_new = attend(info, valid, own, other, by_head, new, lambda c: c)
    parts = merge_twins(info, mine, got, from_new)
    zs = merge_four([parts[0]] + [from_second(parts[SIDE - s], s) for s in (1, 2, 3)])
    rows = merge_final([zs] + [from_first(zs, s) for s in (1, 2, 3)])

    own = [rows] + [from_second(rows, s) for s in (1, 2, 3)]
    other = [from_twin(part) for part in own]
    keep, *sends = project(info, own, other, out_weight)
    total = keep
    for d in (1, 2, 3):
        total = total + from_plane(sends[d - 1], SIDE - d).astype(F32)
    return total.astype(BF16)


def solution(mesh):
    placed = (
        P("ctx", "kvh"),
        P(None, "ctx", "kvh", None),
        P(None, None, "kvh", None),
        P(),
        P("kvh", "ctx"),
    )
    return jax.shard_map(
        on_device, mesh=mesh, in_specs=placed, out_specs=P("kvh", "ctx"), check_vma=False
    )
```

```python
import functools
import math

import jax
import jax.numpy as jnp
from jax import lax
from jax.experimental import pallas as pl
from jax.experimental.pallas import tpu as pltpu
from jax.sharding import PartitionSpec as P

KV_HEADS = 8
QH = 128
HD = 128
REQS = 8
NEW = 32
GROUP = QH // KV_HEADS
SIDE = 4
ROWS = 16
BLOCK = GROUP * ROWS
FEATS = GROUP * HD
WIDE = FEATS + HD
SCALE = HD ** (-0.5) * math.log2(math.e)
EMPTY = -1e30
F32, BF16 = jnp.float32, jnp.bfloat16
MIB = 2**20


def at(z, x, core):
    return ((z % SIDE) * SIDE + x % SIDE) * 2 + core


def places():
    return [(z, x, c) for z in range(SIDE) for x in range(SIDE) for c in range(2)]


def from_first(value, step):
    pairs = [(at(z, x + step, c) if c == 0 else at(z + step, x, c), at(z, x, c)) for z, x, c in places()]
    return lax.ppermute(value, "ctx", pairs)


def from_second(value, step):
    pairs = [(at(z + step, x, c) if c == 0 else at(z, x + step, c), at(z, x, c)) for z, x, c in places()]
    return lax.ppermute(value, "ctx", pairs)


def from_twin(value):
    return lax.ppermute(value, "ctx", [(at(z, x, 1 - c), at(z, x, c)) for z, x, c in places()])


def from_plane(value, step):
    return lax.ppermute(value, "kvh", [((s + step) % SIDE, s) for s in range(SIDE)])


def whole():
    return pl.BlockSpec(memory_space=pltpu.VMEM)


def stack_kernel(*refs):
    for i, ref in enumerate(refs[:-1]):
        refs[-1][i] = ref[...]


def stack(parts):
    return pl.pallas_call(
        stack_kernel,
        out_shape=jax.ShapeDtypeStruct((len(parts), *parts[0].shape), parts[0].dtype),
        in_specs=[whole()] * len(parts),
        out_specs=whole(),
        compiler_params=pltpu.CompilerParams(vmem_limit_bytes=8 * MIB),
        name="stack",
    )(*parts)


def dot_nt(a, b):
    return lax.dot_general(a, b, (((1,), (1,)), ((), ())), preferred_element_type=F32)


def weigh(s):
    most = jnp.max(s, axis=1, keepdims=True)
    w = jnp.exp2((s - most) * SCALE)
    exact = most * SCALE
    top = exact.astype(BF16).astype(F32)
    return top, jnp.exp2(exact - top), jnp.sum(w, axis=1, keepdims=True), w.astype(BF16)


def put_partial(out, index, top, total, summed):
    lane = lax.broadcasted_iota(jnp.int32, (ROWS, HD), 1)
    high = total.astype(BF16).astype(F32)
    low = total - high
    stats = jnp.zeros((ROWS, HD), F32)
    for g in range(GROUP):
        rows = slice(g * ROWS, (g + 1) * ROWS)
        out[index, :, g * HD : (g + 1) * HD] = summed[rows].astype(BF16)
        stats = jnp.where(lane == g, top[rows], stats)
        stats = jnp.where(lane == GROUP + g, high[rows], stats)
        stats = jnp.where(lane == 2 * GROUP + g, low[rows], stats)
    out[index, :, FEATS:] = stats.astype(BF16)


def assemble(info, begin, end, own, other, held):
    z, x, core = info[0], info[1], info[2]
    for dz in range(SIDE):
        plane = (z + dz) % SIDE

        def lay(zeros, ones, dz=dz, plane=plane):
            for dx in range(SIDE):
                zero, one = zeros(dz, dx), ones(dz, dx)
                for head in range(2):
                    for g in range(GROUP):
                        cols = slice(head * FEATS + g * HD, head * FEATS + (g + 1) * HD)
                        pair = jnp.concatenate([zero[:, cols].astype(F32), one[:, cols].astype(F32)], axis=0)
                        held[head, plane * SIDE + (x + dx) % SIDE, g * ROWS : (g + 1) * ROWS, :] = pair.astype(BF16)

        used = jnp.logical_and(2 * plane + 1 >= begin, 2 * plane < end)
        if dz == 0:
            used = True

        @pl.when(jnp.logical_and(used, core == 0))
        def _(lay=lay):
            lay(lambda dz, dx: own[dz][dx], lambda dz, dx: other[dx][dz])

        @pl.when(jnp.logical_and(used, core == 1))
        def _(lay=lay):
            lay(lambda dz, dx: other[dz][dx], lambda dz, dx: own[dx][dz])


def split_heads(cache, held):
    r = lax.broadcasted_iota(jnp.int32, (2 * HD, 2 * HD), 0)
    c = lax.broadcasted_iota(jnp.int32, (2 * HD, 2 * HD), 1)
    pick = (c == jnp.where(r < HD, 2 * r, 2 * (r - HD) + 1)).astype(BF16)
    for i in range(cache.shape[1] // HD):
        rows = slice(i * HD, (i + 1) * HD)
        both = cache[0, rows].reshape(2 * HD, 2 * HD)
        apart = jnp.dot(pick, both, preferred_element_type=F32).astype(BF16)
        held[0, rows] = apart[:HD]
        held[1, rows] = apart[HD:]


def attend_kernel(begin, with_new, info, valid, *refs):
    own, other, cache = refs[:SIDE], refs[SIDE : 2 * SIDE], refs[2 * SIDE]
    refs = refs[2 * SIDE + 1 :]
    if with_new:
        new, sent, mine, new_out, queries, keys = refs
    else:
        sent, mine, queries, keys = refs
    step = pl.program_id(0)
    last = pl.num_programs(0) - 1
    core = info[2]

    @pl.when(step == 0)
    def _():
        assemble(info, begin, begin + pl.num_programs(0), own, other, queries)

    request = begin + step
    count = valid[request]
    slot = cache.shape[1]
    where = [(head, out, half) for head, out in ((1 - core, sent), (core, mine)) for half in range(2)]

    def scores(head, _, half):
        return dot_nt(queries[head, 2 * request + half], keys[head, :, :HD])

    def finish(head, out, half, s):
        top, factor, total, w = weigh(s)
        summed = jnp.dot(w, keys[head, :, HD:], preferred_element_type=F32)
        put_partial(out, half, top, total * factor, summed * factor)

    @pl.when(count >= slot)
    def _():
        split_heads(cache, keys)
        s = scores(*where[0])
        for i, block in enumerate(where):
            later = scores(*where[i + 1]) if i + 1 < len(where) else None
            finish(*block, s)
            s = later

    @pl.when(jnp.logical_and(count > 0, count < slot))
    def _():
        split_heads(cache, keys)
        for block in where:
            s = scores(*block)
            position = lax.broadcasted_iota(jnp.int32, s.shape, 1)
            finish(*block, jnp.where(position < count, s, EMPTY))

    @pl.when(count <= 0)
    def _():
        lane = lax.broadcasted_iota(jnp.int32, (ROWS, WIDE), 1)
        tops = jnp.logical_and(lane >= FEATS, lane < FEATS + GROUP)
        none = jnp.where(tops, EMPTY, 0.0).astype(BF16)
        for _, out, half in where:
            out[half] = none

    if with_new:
        @pl.when(step == last)
        def _():
            z, x = info[0], info[1]
            s = dot_nt(queries[core, z * SIDE + x], new[0, :, :HD])
            token = (x % 2) * ROWS + lax.broadcasted_iota(jnp.int32, s.shape, 0) % ROWS
            key = lax.broadcasted_iota(jnp.int32, s.shape, 1)
            top, factor, total, w = weigh(jnp.where(key <= token, s, EMPTY))
            summed = jnp.dot(w, new[0, :, HD:], preferred_element_type=F32)
            put_partial(new_out, 0, top, total * factor, summed * factor)


def attend(info, valid, own, other, cache, new, begin, count):
    per = cache.shape[1]
    in_specs = [whole()] * (2 * SIDE) + [
        pl.BlockSpec((1, per, 2, 2 * HD), lambda i, info, valid: (begin + i, 0, 0, 0))
    ]
    out_specs = [pl.BlockSpec((2, ROWS, WIDE), lambda i, info, valid: (i, 0, 0))] * 2
    out_shape = [jax.ShapeDtypeStruct((2 * count, ROWS, WIDE), BF16)] * 2
    args = [*own, *other, cache]
    if new is not None:
        in_specs.append(whole())
        out_specs.append(pl.BlockSpec((1, ROWS, WIDE), lambda i, info, valid: (0, 0, 0)))
        out_shape.append(jax.ShapeDtypeStruct((1, ROWS, WIDE), BF16))
        args.append(new)
    return pl.pallas_call(
        functools.partial(attend_kernel, begin, new is not None),
        out_shape=out_shape,
        grid_spec=pltpu.PrefetchScalarGridSpec(
            num_scalar_prefetch=2,
            grid=(count,),
            in_specs=in_specs,
            out_specs=out_specs,
            scratch_shapes=[
                pltpu.VMEM((2, SIDE * SIDE, BLOCK, HD), BF16),
                pltpu.VMEM((2, per, 2 * HD), BF16),
            ],
        ),
        compiler_params=pltpu.CompilerParams(vmem_limit_bytes=50 * MIB),
        cost_estimate=pl.CostEstimate(
            flops=16 * count * BLOCK * per * HD, bytes_accessed=count * per * 4 * HD * 2, transcendentals=0
        ),
        name="attend_new" if new is not None else "attend",
    )(info, valid, *args)


def factors_of(parts):
    stats = [ref[index, :, FEATS:].astype(F32) for ref, index, _ in parts]
    tops = [
        p[:, :GROUP] if counts is None else jnp.where(counts, p[:, :GROUP], EMPTY)
        for p, (_, _, counts) in zip(stats, parts)
    ]
    totals = [p[:, GROUP : 2 * GROUP] + p[:, 2 * GROUP : 3 * GROUP] for p in stats]
    best = functools.reduce(jnp.maximum, tops)
    factors = [
        jnp.exp2(t - best) if counts is None else jnp.where(counts, jnp.exp2(t - best), 0.0)
        for t, (_, _, counts) in zip(tops, parts)
    ]
    return best, sum(f * t for f, t in zip(factors, totals)), factors


def summed_of(parts, factors, g):
    cols = slice(g * HD, (g + 1) * HD)
    return sum(f[:, g : g + 1] * ref[index, :, cols].astype(F32) for f, (ref, index, _) in zip(factors, parts))


def merge_into(jobs):
    ready = [factors_of(parts) for _, _, parts in jobs]
    for (out, index, _), (best, total, _) in zip(jobs, ready):
        high = total.astype(BF16)
        low = (total - high.astype(F32)).astype(BF16)
        rest = jnp.zeros((ROWS, HD - 3 * GROUP), BF16)
        out[index, :, FEATS:] = jnp.concatenate([best.astype(BF16), high, low, rest], axis=1)
    for (out, index, parts), (_, _, factors) in zip(jobs, ready):
        for g in range(GROUP):
            out[index, :, g * HD : (g + 1) * HD] = summed_of(parts, factors, g).astype(BF16)


def twin_kernel(info, *refs):
    mine_parts, got_parts, new = refs[:2], refs[2:4], refs[4]
    outs, (mine, got) = refs[5 : 5 + SIDE], refs[5 + SIDE :]
    for held, parts in ((mine, mine_parts), (got, got_parts)):
        first = 0
        for part in parts:
            held[first : first + part.shape[0]] = part[...]
            first += part.shape[0]
    z, x, core = info[0], info[1], info[2]
    jobs = []
    for d in range(SIDE):
        for j in range(SIDE):
            chip = jnp.where(core == 0, ((z + d) % SIDE) * SIDE + j, j * SIDE + (x + d) % SIDE)
            parts = [(mine, chip, None), (got, chip, None)]
            if d == 0:
                parts.append((new, 0, chip == z * SIDE + x))
            jobs.append((outs[d], j, parts))
    merge_into(jobs)


def merge_twins(info, mine, got, new):
    return pl.pallas_call(
        twin_kernel,
        out_shape=[jax.ShapeDtypeStruct((SIDE, ROWS, WIDE), BF16)] * SIDE,
        in_specs=[pl.BlockSpec(memory_space=pltpu.SMEM)] + [whole()] * 5,
        out_specs=[whole()] * SIDE,
        scratch_shapes=[pltpu.VMEM((SIDE * SIDE, ROWS, WIDE), BF16)] * 2,
        compiler_params=pltpu.CompilerParams(vmem_limit_bytes=24 * MIB),
        name="merge_twins",
    )(info, *mine, *got, new)


def four_kernel(*refs):
    out = refs[-1]
    merge_into([(out, j, [(ref, j, None) for ref in refs[:-1]]) for j in range(SIDE)])


def merge_four(parts):
    return pl.pallas_call(
        four_kernel,
        out_shape=jax.ShapeDtypeStruct((SIDE, ROWS, WIDE), BF16),
        in_specs=[whole()] * SIDE,
        out_specs=whole(),
        compiler_params=pltpu.CompilerParams(vmem_limit_bytes=24 * MIB),
        name="merge_four",
    )(*parts)


def final_kernel(*refs):
    out = refs[-1]
    blocks = [[(ref, j, None) for ref in refs[:-1]] for j in range(SIDE)]
    ready = []
    for parts in blocks:
        _, total, factors = factors_of(parts)
        ready.append([f / total for f in factors])
    for j, (parts, factors) in enumerate(zip(blocks, ready)):
        for g in range(GROUP):
            out[j, :, g * HD : (g + 1) * HD] = summed_of(parts, factors, g).astype(BF16)


def merge_final(parts):
    return pl.pallas_call(
        final_kernel,
        out_shape=jax.ShapeDtypeStruct((SIDE, ROWS, FEATS), BF16),
        in_specs=[whole()] * SIDE,
        out_specs=whole(),
        compiler_params=pltpu.CompilerParams(vmem_limit_bytes=24 * MIB),
        name="merge_final",
    )(*parts)


def project_kernel(info, *refs):
    own, other, weight = refs[:SIDE], refs[SIDE : 2 * SIDE], refs[2 * SIDE]
    keep, sends, held, acc = refs[2 * SIDE + 1], refs[2 * SIDE + 2 : 3 * SIDE + 1], refs[-2], refs[-1]
    step = pl.program_id(0)
    z, x, core, y = info[0], info[1], info[2], info[3]
    depth = weight.shape[0]
    per = FEATS // depth

    @pl.when(step == 0)
    def _():
        acc[...] = jnp.zeros_like(acc)

        def place(zero, one):
            for d in range(SIDE):
                for j in range(SIDE):
                    for half, values, chip in (
                        (0, zero, ((z + d) % SIDE) * SIDE + j),
                        (1, one, j * SIDE + (x + d) % SIDE),
                    ):
                        rows = pl.ds(pl.multiple_of(chip * ROWS, ROWS), ROWS)
                        for k in range(per):
                            held[half * per + k, rows, :] = values[d][j, :, k * depth : (k + 1) * depth]

        @pl.when(core == 0)
        def _():
            place(own, other)

        @pl.when(core == 1)
        def _():
            place(other, own)

    acc[...] += jnp.dot(held[step], weight[...], preferred_element_type=F32)

    @pl.when(step == pl.num_programs(0) - 1)
    def _():
        count = keep.shape[0]
        for d in range(SIDE):
            rows = acc[pl.ds(pl.multiple_of(((y + d) % SIDE) * count, count), count), :]
            if d == 0:
                keep[...] = rows
            else:
                sends[d - 1][...] = rows.astype(BF16)


def project(info, own, other, weight):
    depth = 1024
    cols = weight.shape[1]
    rows = SIDE * SIDE * ROWS
    return pl.pallas_call(
        project_kernel,
        out_shape=[jax.ShapeDtypeStruct((rows // SIDE, cols), F32)]
        + [jax.ShapeDtypeStruct((rows // SIDE, cols), BF16)] * (SIDE - 1),
        grid=(weight.shape[0] // depth,),
        in_specs=[pl.BlockSpec(memory_space=pltpu.SMEM)]
        + [whole()] * (2 * SIDE)
        + [pl.BlockSpec((depth, cols), lambda i: (i, 0))],
        out_specs=[whole()] * SIDE,
        scratch_shapes=[
            pltpu.VMEM((weight.shape[0] // depth, rows, depth), BF16),
            pltpu.VMEM((rows, cols), F32),
        ],
        compiler_params=pltpu.CompilerParams(vmem_limit_bytes=32 * MIB),
        name="project",
    )(info, *own, *other, weight)


def on_device(queries, cache, new_kv, lengths, out_weight):
    index = lax.axis_index("ctx")
    z, x, core = index // (2 * SIDE), (index // 2) % SIDE, index % 2
    info = jnp.stack([z, x, core, lax.axis_index("kvh")]).astype(jnp.int32)
    slot = cache.shape[1]
    valid = jnp.clip(lengths - index * slot, 0, slot).astype(jnp.int32)

    request = 2 * z + x // 2
    new = lax.dynamic_slice(new_kv, (request, 0, core, 0), (1, NEW, 1, 2 * HD)).reshape(1, NEW, 2 * HD)
    line = stack([queries] + [from_first(queries, s) for s in (1, 2, 3)])
    info, valid, new, line = lax.optimization_barrier((info, valid, new, line))
    own = [line] + [from_second(line, s) for s in (1, 2, 3)]
    other = [from_twin(part) for part in own]

    early = REQS - 2
    sent0, mine0 = attend(info, valid, own, other, cache, None, 0, early)
    got0 = from_twin(sent0)
    sent1, mine1, from_new = attend(info, valid, own, other, cache, new, early, REQS - early)
    parts = merge_twins(info, [mine0, mine1], [got0, from_twin(sent1)], from_new)
    zs = merge_four([parts[0]] + [from_second(parts[SIDE - s], s) for s in (1, 2, 3)])
    rows = merge_final([zs] + [from_first(zs, s) for s in (1, 2, 3)])

    own = [rows] + [from_second(rows, s) for s in (1, 2, 3)]
    other = [from_twin(part) for part in own]
    keep, *sends = project(info, own, other, out_weight)
    total = keep
    for d in (1, 2, 3):
        total = total + from_plane(sends[d - 1], SIDE - d).astype(F32)
    return total.astype(BF16)


def solution(mesh):
    placed = (
        P("ctx", "kvh"),
        P(None, "ctx", "kvh", None),
        P(None, None, "kvh", None),
        P(),
        P("kvh", "ctx"),
    )
    return jax.shard_map(
        on_device, mesh=mesh, in_specs=placed, out_specs=P("kvh", "ctx"), check_vma=False
    )
```

```python
import functools
import math

import jax
import jax.numpy as jnp
from jax import lax
from jax.experimental import pallas as pl
from jax.experimental.pallas import tpu as pltpu
from jax.sharding import PartitionSpec as P

KV_HEADS = 8
QH = 128
HD = 128
REQS = 8
NEW = 32
GROUP = QH // KV_HEADS
AHEAD = 4
SIDE = 4
ROWS = 16
BLOCK = GROUP * ROWS
FEATS = GROUP * HD
WIDE = FEATS + HD
SCALE = HD ** (-0.5) * math.log2(math.e)
EMPTY = -1e30
F32, BF16 = jnp.float32, jnp.bfloat16
MIB = 2**20


def at(z, x, core):
    return ((z % SIDE) * SIDE + x % SIDE) * 2 + core


def places():
    return [(z, x, c) for z in range(SIDE) for x in range(SIDE) for c in range(2)]


def from_first(value, step):
    pairs = [(at(z, x + step, c) if c == 0 else at(z + step, x, c), at(z, x, c)) for z, x, c in places()]
    return lax.ppermute(value, "ctx", pairs)


def from_second(value, step):
    pairs = [(at(z + step, x, c) if c == 0 else at(z, x + step, c), at(z, x, c)) for z, x, c in places()]
    return lax.ppermute(value, "ctx", pairs)


def from_twin(value):
    return lax.ppermute(value, "ctx", [(at(z, x, 1 - c), at(z, x, c)) for z, x, c in places()])


def from_plane(value, step):
    return lax.ppermute(value, "kvh", [((s + step) % SIDE, s) for s in range(SIDE)])


def whole():
    return pl.BlockSpec(memory_space=pltpu.VMEM)


def stack_kernel(*refs):
    for i, ref in enumerate(refs[:-1]):
        refs[-1][i] = ref[...]


def stack(parts):
    return pl.pallas_call(
        stack_kernel,
        out_shape=jax.ShapeDtypeStruct((len(parts), *parts[0].shape), parts[0].dtype),
        in_specs=[whole()] * len(parts),
        out_specs=whole(),
        compiler_params=pltpu.CompilerParams(vmem_limit_bytes=8 * MIB),
        name="stack",
    )(*parts)


def dot_nt(a, b):
    return lax.dot_general(a, b, (((1,), (1,)), ((), ())), preferred_element_type=F32)


def weigh(s):
    top = jnp.max(s, axis=1, keepdims=True)
    w = jnp.exp2((s - top) * SCALE)
    return top, jnp.sum(w, axis=1, keepdims=True), w.astype(BF16)


def in_parts(value, count):
    parts = []
    for _ in range(count):
        part = value.astype(BF16)
        parts.append(part)
        value = value - part.astype(F32)
    return parts


def pack_stats(top, total):
    rest = jnp.zeros((ROWS, HD - 5 * GROUP), BF16)
    return jnp.concatenate([*in_parts(top, 3), *in_parts(total, 2), rest], axis=1)


def unpack_stats(tile):
    parts = [tile[:, i * GROUP : (i + 1) * GROUP].astype(F32) for i in range(5)]
    return (parts[0] + parts[1]) + parts[2], parts[3] + parts[4]


def put_partial(out, index, top, total, summed):
    lane = lax.broadcasted_iota(jnp.int32, (ROWS, HD), 1)
    tops = totals = jnp.zeros((ROWS, HD), F32)
    for g in range(GROUP):
        rows = slice(g * ROWS, (g + 1) * ROWS)
        out[index, :, g * HD : (g + 1) * HD] = summed[rows].astype(BF16)
        tops = jnp.where(lane == g, top[rows], tops)
        totals = jnp.where(lane == g, total[rows], totals)
    out[index, :, FEATS:] = pack_stats(tops[:, :GROUP], totals[:, :GROUP])


def assemble(info, own, other, held):
    z, x, core = info[0], info[1], info[2]
    for dz in range(SIDE):
        plane = (z + dz) % SIDE

        def lay(zeros, ones, dz=dz, plane=plane):
            for dx in range(SIDE):
                zero, one = zeros(dz, dx), ones(dz, dx)
                for head in range(2):
                    for g in range(GROUP):
                        cols = slice(head * FEATS + g * HD, head * FEATS + (g + 1) * HD)
                        pair = jnp.concatenate([zero[:, cols].astype(F32), one[:, cols].astype(F32)], axis=0)
                        held[head, plane * SIDE + (x + dx) % SIDE, g * ROWS : (g + 1) * ROWS, :] = pair.astype(BF16)

        @pl.when(core == 0)
        def _(lay=lay):
            lay(lambda dz, dx: own[dz][dx], lambda dz, dx: other[dx][dz])

        @pl.when(core == 1)
        def _(lay=lay):
            lay(lambda dz, dx: other[dz][dx], lambda dz, dx: own[dx][dz])


def split_heads(cache, at, out):
    r = lax.broadcasted_iota(jnp.int32, (2 * HD, 2 * HD), 0)
    c = lax.broadcasted_iota(jnp.int32, (2 * HD, 2 * HD), 1)
    pick = (c == jnp.where(r < HD, 2 * r, 2 * (r - HD) + 1)).astype(BF16)
    for i in range(cache.shape[1] // HD):
        rows = slice(i * HD, (i + 1) * HD)
        both = cache[at, rows].reshape(2 * HD, 2 * HD)
        apart = jnp.dot(pick, both, preferred_element_type=F32).astype(BF16)
        out(0, rows, apart[:HD])
        out(1, rows, apart[HD:])


def ahead_kernel(cache, *refs):
    out = refs[-1]

    def put(head, rows, value):
        out[0, head, rows] = value

    split_heads(cache, 0, put)


def split_ahead(cache, held, begin, count):
    per = cache.shape[1]
    return pl.pallas_call(
        ahead_kernel,
        grid=(count,),
        in_specs=[pl.BlockSpec((1, per, 2, 2 * HD), lambda i: (begin + i, 0, 0, 0))]
        + ([] if held is None else [pl.BlockSpec(memory_space=pl.ANY)]),
        out_specs=pl.BlockSpec((1, 2, per, 2 * HD), lambda i: (begin + i, 0, 0, 0)),
        out_shape=jax.ShapeDtypeStruct((AHEAD, 2, per, 2 * HD), BF16),
        input_output_aliases={} if held is None else {1: 0},
        compiler_params=pltpu.CompilerParams(vmem_limit_bytes=54 * MIB),
        cost_estimate=pl.CostEstimate(flops=0, bytes_accessed=count * 8 * MIB, transcendentals=0),
        name="split_ahead",
    )(cache, *([] if held is None else [held]))


def attend_kernel(info, valid, *refs):
    own, other, ahead, cache, new = refs[:SIDE], refs[SIDE : 2 * SIDE], *refs[2 * SIDE : 2 * SIDE + 3]
    sent, mine, new_out, queries, keys, held, arrived = refs[2 * SIDE + 3 :]
    step = pl.program_id(0)
    last = pl.num_programs(0) - 1
    core = info[2]
    slot = cache.shape[1]
    side = step % 2

    def fetch(request):
        if request < AHEAD:
            return pltpu.make_async_copy(
                ahead.at[request], keys.at[request // 2 % 2, request % 2], arrived.at[request]
            )
        return pltpu.make_async_copy(cache.at[request], held.at[request - AHEAD], arrived.at[request])

    @pl.when(step == 0)
    def _():
        for request in range(REQS):
            fetch(request).start()
        assemble(info, own, other, queries)

    for now in range(REQS // 2):

        @pl.when(step == now)
        def _(now=now):
            for r in range(2):
                fetch(2 * now + r).wait()

    @pl.when(2 * step >= AHEAD)
    def _():
        for r in range(2):

            def put(head, rows, value, r=r):
                keys[side, r, head, rows] = value

            split_heads(held, 2 * step - AHEAD + r, put)

    first, second = valid[2 * step], valid[2 * step + 1]
    where = [
        (r, head, out, half)
        for r in range(2)
        for head, out in ((1 - core, sent), (core, mine))
        for half in range(2)
    ]

    def scores(r, head, _, half):
        return dot_nt(queries[head, 4 * step + 2 * r + half], keys[side, r, head, :, :HD])

    def finish(r, head, out, half, s):
        top, total, w = weigh(s)
        summed = jnp.dot(w, keys[side, r, head, :, HD:], preferred_element_type=F32)
        put_partial(out, 2 * r + half, top, total, summed)

    full = jnp.logical_and(first >= slot, second >= slot)

    @pl.when(full)
    def _():
        s = scores(*where[0])
        for i, block in enumerate(where):
            later = scores(*where[i + 1]) if i + 1 < len(where) else None
            finish(*block, s)
            s = later

    @pl.when(jnp.logical_not(full))
    def _():
        @pl.loop(0, 2)
        def _(r):
            count = valid[2 * step + r]

            @pl.when(count > 0)
            def _():
                for head, out in ((1 - core, sent), (core, mine)):

                    @pl.loop(0, 2)
                    def _(half, head=head, out=out):
                        s = scores(r, head, out, half)
                        position = lax.broadcasted_iota(jnp.int32, s.shape, 1)
                        finish(r, head, out, half, jnp.where(position < count, s, EMPTY))

            @pl.when(count <= 0)
            def _():
                none = pack_stats(jnp.full((ROWS, GROUP), EMPTY, F32), jnp.zeros((ROWS, GROUP), F32))
                for out in (sent, mine):
                    for half in range(2):
                        out[2 * r + half, :, :FEATS] = jnp.zeros((ROWS, FEATS), BF16)
                        out[2 * r + half, :, FEATS:] = none

    @pl.when(step == last)
    def _():
        z, x = info[0], info[1]
        s = dot_nt(queries[core, z * SIDE + x], new[0, :, :HD])
        token = (x % 2) * ROWS + lax.broadcasted_iota(jnp.int32, s.shape, 0) % ROWS
        key = lax.broadcasted_iota(jnp.int32, s.shape, 1)
        top, total, w = weigh(jnp.where(key <= token, s, EMPTY))
        summed = jnp.dot(w, new[0, :, HD:], preferred_element_type=F32)
        put_partial(new_out, 0, top, total, summed)


def attend(info, valid, own, other, ahead, cache, new):
    reqs, per = cache.shape[:2]
    blocks = jax.ShapeDtypeStruct((2 * reqs, ROWS, WIDE), BF16)
    return pl.pallas_call(
        attend_kernel,
        out_shape=[blocks, blocks, jax.ShapeDtypeStruct((1, ROWS, WIDE), BF16)],
        grid_spec=pltpu.PrefetchScalarGridSpec(
            num_scalar_prefetch=2,
            grid=(reqs // 2,),
            in_specs=[whole()] * (2 * SIDE) + [pl.BlockSpec(memory_space=pl.ANY)] * 2 + [whole()],
            out_specs=[pl.BlockSpec((4, ROWS, WIDE), lambda i, info, valid: (i, 0, 0))] * 2
            + [pl.BlockSpec((1, ROWS, WIDE), lambda i, info, valid: (0, 0, 0))],
            scratch_shapes=[
                pltpu.VMEM((2, SIDE * SIDE, BLOCK, HD), BF16),
                pltpu.VMEM((2, 2, 2, per, 2 * HD), BF16),
                pltpu.VMEM((REQS - AHEAD, *cache.shape[1:]), BF16),
                pltpu.SemaphoreType.DMA((REQS,)),
            ],
        ),
        compiler_params=pltpu.CompilerParams(vmem_limit_bytes=46 * MIB),
        cost_estimate=pl.CostEstimate(
            flops=16 * reqs * BLOCK * per * HD, bytes_accessed=reqs * per * 4 * HD * 2, transcendentals=0
        ),
        name="attend",
    )(info, valid, *own, *other, ahead, cache, new)


def factors_of(parts):
    stats = [unpack_stats(ref[index, :, FEATS:]) for ref, index, _ in parts]
    tops = [top if counts is None else jnp.where(counts, top, EMPTY) for (top, _), (_, _, counts) in zip(stats, parts)]
    best = functools.reduce(jnp.maximum, tops)
    factors = [jnp.exp2((top - best) * SCALE) for top in tops]
    factors = [f if counts is None else jnp.where(counts, f, 0.0) for f, (_, _, counts) in zip(factors, parts)]
    return best, sum(f * total for f, (_, total) in zip(factors, stats)), factors


def summed_of(parts, factors, g):
    cols = slice(g * HD, (g + 1) * HD)
    return sum(f[:, g : g + 1] * ref[index, :, cols].astype(F32) for f, (ref, index, _) in zip(factors, parts))


def merge_into(jobs):
    ready = [factors_of(parts) for _, _, parts in jobs]
    for (out, index, _), (best, total, _) in zip(jobs, ready):
        out[index, :, FEATS:] = pack_stats(best, total)
    for (out, index, parts), (_, _, factors) in zip(jobs, ready):
        for g in range(GROUP):
            out[index, :, g * HD : (g + 1) * HD] = summed_of(parts, factors, g).astype(BF16)


def twin_kernel(info, mine, got, new, *outs):
    z, x, core = info[0], info[1], info[2]
    jobs = []
    for d in range(SIDE):
        for j in range(SIDE):
            chip = jnp.where(core == 0, ((z + d) % SIDE) * SIDE + j, j * SIDE + (x + d) % SIDE)
            parts = [(mine, chip, None), (got, chip, None)]
            if d == 0:
                parts.append((new, 0, chip == z * SIDE + x))
            jobs.append((outs[d], j, parts))
    merge_into(jobs)


def merge_twins(info, mine, got, new):
    return pl.pallas_call(
        twin_kernel,
        out_shape=[jax.ShapeDtypeStruct((SIDE, ROWS, WIDE), BF16)] * SIDE,
        in_specs=[pl.BlockSpec(memory_space=pltpu.SMEM)] + [whole()] * 3,
        out_specs=[whole()] * SIDE,
        compiler_params=pltpu.CompilerParams(vmem_limit_bytes=24 * MIB),
        name="merge_twins",
    )(info, mine, got, new)


def four_kernel(*refs):
    out = refs[-1]
    merge_into([(out, j, [(ref, j, None) for ref in refs[:-1]]) for j in range(SIDE)])


def merge_four(parts):
    return pl.pallas_call(
        four_kernel,
        out_shape=jax.ShapeDtypeStruct((SIDE, ROWS, WIDE), BF16),
        in_specs=[whole()] * SIDE,
        out_specs=whole(),
        compiler_params=pltpu.CompilerParams(vmem_limit_bytes=24 * MIB),
        name="merge_four",
    )(*parts)


def final_kernel(*refs):
    out = refs[-1]
    blocks = [[(ref, j, None) for ref in refs[:-1]] for j in range(SIDE)]
    ready = []
    for parts in blocks:
        _, total, factors = factors_of(parts)
        ready.append([f / total for f in factors])
    for j, (parts, factors) in enumerate(zip(blocks, ready)):
        for g in range(GROUP):
            out[j, :, g * HD : (g + 1) * HD] = summed_of(parts, factors, g).astype(BF16)


def merge_final(parts):
    return pl.pallas_call(
        final_kernel,
        out_shape=jax.ShapeDtypeStruct((SIDE, ROWS, FEATS), BF16),
        in_specs=[whole()] * SIDE,
        out_specs=whole(),
        compiler_params=pltpu.CompilerParams(vmem_limit_bytes=24 * MIB),
        name="merge_final",
    )(*parts)


def project_kernel(info, *refs):
    own, other, weight = refs[:SIDE], refs[SIDE : 2 * SIDE], refs[2 * SIDE]
    keep, sends, held, acc = refs[2 * SIDE + 1], refs[2 * SIDE + 2 : 3 * SIDE + 1], refs[-2], refs[-1]
    step = pl.program_id(0)
    z, x, core, y = info[0], info[1], info[2], info[3]
    depth = weight.shape[0]
    per = FEATS // depth

    @pl.when(step == 0)
    def _():
        acc[...] = jnp.zeros_like(acc)

        def place(zero, one):
            for d in range(SIDE):
                for j in range(SIDE):
                    for half, values, chip in (
                        (0, zero, ((z + d) % SIDE) * SIDE + j),
                        (1, one, j * SIDE + (x + d) % SIDE),
                    ):
                        rows = pl.ds(pl.multiple_of(chip * ROWS, ROWS), ROWS)
                        for k in range(per):
                            held[half * per + k, rows, :] = values[d][j, :, k * depth : (k + 1) * depth]

        @pl.when(core == 0)
        def _():
            place(own, other)

        @pl.when(core == 1)
        def _():
            place(other, own)

    acc[...] += jnp.dot(held[step], weight[...], preferred_element_type=F32)

    @pl.when(step == pl.num_programs(0) - 1)
    def _():
        count = keep.shape[0]
        for d in range(SIDE):
            rows = acc[pl.ds(pl.multiple_of(((y + d) % SIDE) * count, count), count), :]
            if d == 0:
                keep[...] = rows
            else:
                sends[d - 1][...] = rows.astype(BF16)


def project(info, own, other, weight):
    depth = 1024
    cols = weight.shape[1]
    rows = SIDE * SIDE * ROWS
    return pl.pallas_call(
        project_kernel,
        out_shape=[jax.ShapeDtypeStruct((rows // SIDE, cols), F32)]
        + [jax.ShapeDtypeStruct((rows // SIDE, cols), BF16)] * (SIDE - 1),
        grid=(weight.shape[0] // depth,),
        in_specs=[pl.BlockSpec(memory_space=pltpu.SMEM)]
        + [whole()] * (2 * SIDE)
        + [pl.BlockSpec((depth, cols), lambda i: (i, 0))],
        out_specs=[whole()] * SIDE,
        scratch_shapes=[
            pltpu.VMEM((weight.shape[0] // depth, rows, depth), BF16),
            pltpu.VMEM((rows, cols), F32),
        ],
        compiler_params=pltpu.CompilerParams(vmem_limit_bytes=32 * MIB),
        name="project",
    )(info, *own, *other, weight)


def on_device(queries, cache, new_kv, lengths, out_weight):
    index = lax.axis_index("ctx")
    z, x, core = index // (2 * SIDE), (index // 2) % SIDE, index % 2
    info = jnp.stack([z, x, core, lax.axis_index("kvh")]).astype(jnp.int32)
    slot = cache.shape[1]
    valid = jnp.clip(lengths - index * slot, 0, slot).astype(jnp.int32)

    request = 2 * z + x // 2
    new = lax.dynamic_slice(new_kv, (request, 0, core, 0), (1, NEW, 1, 2 * HD)).reshape(1, NEW, 2 * HD)
    ahead = split_ahead(cache, None, 0, 1)
    line = stack([queries] + [from_first(queries, s) for s in (1, 2, 3)])
    info, valid, new, line, ahead = lax.optimization_barrier((info, valid, new, line, ahead))
    own = [line] + [from_second(line, s) for s in (1, 2, 3)]
    ahead = split_ahead(cache, ahead, 1, AHEAD - 1)
    *own, ahead = lax.optimization_barrier((*own, ahead))
    other = [from_twin(part) for part in own]

    sent, mine, from_new = attend(info, valid, own, other, ahead, cache, new)
    parts = merge_twins(info, mine, from_twin(sent), from_new)
    zs = merge_four([parts[0]] + [from_second(parts[SIDE - s], s) for s in (1, 2, 3)])
    rows = merge_final([zs] + [from_first(zs, s) for s in (1, 2, 3)])

    own = [rows] + [from_second(rows, s) for s in (1, 2, 3)]
    other = [from_twin(part) for part in own]
    keep, *sends = project(info, own, other, out_weight)
    total = keep
    for d in (1, 2, 3):
        total = total + from_plane(sends[d - 1], SIDE - d).astype(F32)
    return total.astype(BF16)


def solution(mesh):
    placed = (
        P("ctx", "kvh"),
        P(None, "ctx", "kvh", None),
        P(None, None, "kvh", None),
        P(),
        P("kvh", "ctx"),
    )
    return jax.shard_map(
        on_device, mesh=mesh, in_specs=placed, out_specs=P("kvh", "ctx"), check_vma=False
    )
```

```python
import functools
import math

import jax
import jax.numpy as jnp
from jax import lax
from jax.experimental import pallas as pl
from jax.experimental.pallas import tpu as pltpu
from jax.sharding import PartitionSpec as P

KV_HEADS = 8
QH = 128
HD = 128
REQS = 8
NEW = 32
GROUP = QH // KV_HEADS
AHEAD = 4
SIDE = 4
ROWS = 16
BLOCK = GROUP * ROWS
FEATS = GROUP * HD
WIDE = FEATS + HD
SCALE = HD ** (-0.5) * math.log2(math.e)
EMPTY = -1e30
F32, BF16 = jnp.float32, jnp.bfloat16
MIB = 2**20


def at(z, x, core):
    return ((z % SIDE) * SIDE + x % SIDE) * 2 + core


def places():
    return [(z, x, c) for z in range(SIDE) for x in range(SIDE) for c in range(2)]


def from_first(value, step):
    pairs = [(at(z, x + step, c) if c == 0 else at(z + step, x, c), at(z, x, c)) for z, x, c in places()]
    return lax.ppermute(value, "ctx", pairs)


def from_second(value, step):
    pairs = [(at(z + step, x, c) if c == 0 else at(z, x + step, c), at(z, x, c)) for z, x, c in places()]
    return lax.ppermute(value, "ctx", pairs)


def from_twin(value):
    return lax.ppermute(value, "ctx", [(at(z, x, 1 - c), at(z, x, c)) for z, x, c in places()])


def from_plane(value, step):
    return lax.ppermute(value, "kvh", [((s + step) % SIDE, s) for s in range(SIDE)])


def whole():
    return pl.BlockSpec(memory_space=pltpu.VMEM)


def stack_kernel(*refs):
    for i, ref in enumerate(refs[:-1]):
        refs[-1][i] = ref[...]


def stack(parts):
    return pl.pallas_call(
        stack_kernel,
        out_shape=jax.ShapeDtypeStruct((len(parts), *parts[0].shape), parts[0].dtype),
        in_specs=[whole()] * len(parts),
        out_specs=whole(),
        compiler_params=pltpu.CompilerParams(vmem_limit_bytes=8 * MIB),
        name="stack",
    )(*parts)


def dot_nt(a, b):
    return lax.dot_general(a, b, (((1,), (1,)), ((), ())), preferred_element_type=F32)


def weigh(s):
    top = jnp.max(s, axis=1, keepdims=True)
    return top, jnp.exp2((s - top) * SCALE).astype(BF16)


def sum_up(w, values):
    ones = jnp.ones(values.shape, BF16)
    both = jnp.dot(w, jnp.concatenate([values, ones], axis=1), preferred_element_type=F32)
    return both[:, :HD], both[:, HD:]


def in_parts(value, count):
    parts = []
    for _ in range(count):
        part = value.astype(BF16)
        parts.append(part)
        value = value - part.astype(F32)
    return parts


def pack_stats(top, total):
    rest = jnp.zeros((ROWS, HD - 5 * GROUP), BF16)
    return jnp.concatenate([*in_parts(top, 3), *in_parts(total, 2), rest], axis=1)


def put_partial(out, index, top, summed, total):
    lane = lax.broadcasted_iota(jnp.int32, (ROWS, HD), 1)
    tops = totals = jnp.zeros((ROWS, HD), F32)
    for g in range(GROUP):
        rows = slice(g * ROWS, (g + 1) * ROWS)
        out[index, :, g * HD : (g + 1) * HD] = summed[rows].astype(BF16)
        tops = jnp.where(lane == g, top[rows], tops)
        totals = jnp.where(lane == g, total[rows], totals)
    out[index, :, FEATS:] = pack_stats(tops[:, :GROUP], totals[:, :GROUP])


def assemble(info, own, other, held):
    z, x, core = info[0], info[1], info[2]
    for dz in range(SIDE):
        plane = (z + dz) % SIDE

        def lay(zeros, ones, dz=dz, plane=plane):
            for dx in range(SIDE):
                zero, one = zeros(dz, dx), ones(dz, dx)
                for head in range(2):
                    for g in range(GROUP):
                        cols = slice(head * FEATS + g * HD, head * FEATS + (g + 1) * HD)
                        pair = jnp.concatenate([zero[:, cols].astype(F32), one[:, cols].astype(F32)], axis=0)
                        held[head, plane * SIDE + (x + dx) % SIDE, g * ROWS : (g + 1) * ROWS, :] = pair.astype(BF16)

        @pl.when(core == 0)
        def _(lay=lay):
            lay(lambda dz, dx: own[dz][dx], lambda dz, dx: other[dx][dz])

        @pl.when(core == 1)
        def _(lay=lay):
            lay(lambda dz, dx: other[dz][dx], lambda dz, dx: own[dx][dz])


def split_heads(cache, at, out):
    r = lax.broadcasted_iota(jnp.int32, (2 * HD, 2 * HD), 0)
    c = lax.broadcasted_iota(jnp.int32, (2 * HD, 2 * HD), 1)
    pick = (c == jnp.where(r < HD, 2 * r, 2 * (r - HD) + 1)).astype(BF16)
    for i in range(cache.shape[1] // HD):
        rows = slice(i * HD, (i + 1) * HD)
        both = cache[at, rows].reshape(2 * HD, 2 * HD)
        apart = jnp.dot(pick, both, preferred_element_type=F32).astype(BF16)
        out(0, rows, apart[:HD])
        out(1, rows, apart[HD:])


def ahead_kernel(cache, *refs):
    out = refs[-1]

    def put(head, rows, value):
        out[0, head, rows] = value

    split_heads(cache, 0, put)


def split_ahead(cache, held, begin, count):
    per = cache.shape[1]
    return pl.pallas_call(
        ahead_kernel,
        grid=(count,),
        in_specs=[pl.BlockSpec((1, per, 2, 2 * HD), lambda i: (begin + i, 0, 0, 0))]
        + ([] if held is None else [pl.BlockSpec(memory_space=pl.ANY)]),
        out_specs=pl.BlockSpec((1, 2, per, 2 * HD), lambda i: (begin + i, 0, 0, 0)),
        out_shape=jax.ShapeDtypeStruct((AHEAD, 2, per, 2 * HD), BF16),
        input_output_aliases={} if held is None else {1: 0},
        compiler_params=pltpu.CompilerParams(vmem_limit_bytes=54 * MIB),
        cost_estimate=pl.CostEstimate(flops=0, bytes_accessed=count * 8 * MIB, transcendentals=0),
        name="split_ahead",
    )(cache, *([] if held is None else [held]))


def attend_kernel(info, valid, *refs):
    own, other, ahead, cache, new = refs[:SIDE], refs[SIDE : 2 * SIDE], *refs[2 * SIDE : 2 * SIDE + 3]
    sent, mine, queries, keys, held, mine_new, arrived = refs[2 * SIDE + 3 :]
    step = pl.program_id(0)
    core = info[2]
    slot = cache.shape[1]
    side = step % 2

    def fetch(request):
        if request < AHEAD:
            return pltpu.make_async_copy(
                ahead.at[request], keys.at[request // 2 % 2, request % 2], arrived.at[request]
            )
        return pltpu.make_async_copy(cache.at[request], held.at[request - AHEAD], arrived.at[request])

    @pl.when(step == 0)
    def _():
        for request in range(2):
            fetch(request).start()
        assemble(info, own, other, queries)

    for now in range(REQS // 2):

        @pl.when(step == now)
        def _(now=now):
            for r in range(2):
                fetch(2 * now + r).wait()
            if now == 0:
                for request in range(2, REQS):
                    fetch(request).start()

    for r in range(2):

        @pl.when(2 * step + r >= AHEAD)
        def _(r=r):
            def put(head, rows, value):
                keys[side, r, head, rows] = value

            split_heads(held, 2 * step + r - AHEAD, put)

    first, second = valid[2 * step], valid[2 * step + 1]
    where = [
        (r, head, out, half)
        for r in range(2)
        for head, out in ((1 - core, sent), (core, mine))
        for half in range(2)
    ]

    def scores(r, head, _, half):
        return dot_nt(queries[head, 4 * step + 2 * r + half], keys[side, r, head, :, :HD])

    def finish(r, head, out, half, s):
        top, w = weigh(s)
        put_partial(out, 2 * r + half, top, *sum_up(w, keys[side, r, head, :, HD:]))

    full = jnp.logical_and(first >= slot, second >= slot)

    @pl.when(full)
    def _():
        s = scores(*where[0])
        for i, block in enumerate(where):
            later = scores(*where[i + 1]) if i + 1 < len(where) else None
            finish(*block, s)
            s = later

    @pl.when(jnp.logical_not(full))
    def _():
        @pl.loop(0, 2)
        def _(r):
            count = valid[2 * step + r]

            @pl.when(count > 0)
            def _():
                for head, out in ((1 - core, sent), (core, mine)):

                    @pl.loop(0, 2)
                    def _(half, head=head, out=out):
                        s = scores(r, head, out, half)
                        position = lax.broadcasted_iota(jnp.int32, s.shape, 1)
                        finish(r, head, out, half, jnp.where(position < count, s, EMPTY))

            @pl.when(count <= 0)
            def _():
                none = pack_stats(jnp.full((ROWS, GROUP), EMPTY, F32), jnp.zeros((ROWS, GROUP), F32))
                for out in (sent, mine):
                    for half in range(2):
                        out[2 * r + half, :, :FEATS] = jnp.zeros((ROWS, FEATS), BF16)
                        out[2 * r + half, :, FEATS:] = none

    z, x = info[0], info[1]

    @pl.when(step == z)
    def _():
        s = dot_nt(queries[core, z * SIDE + x], new[0, :, :HD])
        token = (x % 2) * ROWS + lax.broadcasted_iota(jnp.int32, s.shape, 0) % ROWS
        key = lax.broadcasted_iota(jnp.int32, s.shape, 1)
        top, w = weigh(jnp.where(key <= token, s, EMPTY))
        put_partial(mine_new, 0, top, *sum_up(w, new[0, :, HD:]))
        merge_into([(mine, x)], [[(mine, x)], [(mine_new, 0)]])


def attend(info, valid, own, other, ahead, cache, new):
    reqs, per = cache.shape[:2]
    blocks = jax.ShapeDtypeStruct((2 * reqs, ROWS, WIDE), BF16)
    return pl.pallas_call(
        attend_kernel,
        out_shape=[blocks, blocks],
        grid_spec=pltpu.PrefetchScalarGridSpec(
            num_scalar_prefetch=2,
            grid=(reqs // 2,),
            in_specs=[whole()] * (2 * SIDE) + [pl.BlockSpec(memory_space=pl.ANY)] * 2 + [whole()],
            out_specs=[pl.BlockSpec((4, ROWS, WIDE), lambda i, info, valid: (i, 0, 0))] * 2,
            scratch_shapes=[
                pltpu.VMEM((2, SIDE * SIDE, BLOCK, HD), BF16),
                pltpu.VMEM((2, 2, 2, per, 2 * HD), BF16),
                pltpu.VMEM((REQS - AHEAD, *cache.shape[1:]), BF16),
                pltpu.VMEM((1, ROWS, WIDE), BF16),
                pltpu.SemaphoreType.DMA((REQS,)),
            ],
        ),
        compiler_params=pltpu.CompilerParams(vmem_limit_bytes=46 * MIB),
        cost_estimate=pl.CostEstimate(
            flops=16 * reqs * BLOCK * per * HD, bytes_accessed=reqs * per * 4 * HD * 2, transcendentals=0
        ),
        name="attend",
    )(info, valid, *own, *other, ahead, cache, new)


def zero_one(shape, test):
    return test(lax.broadcasted_iota(jnp.int32, shape, 0), lax.broadcasted_iota(jnp.int32, shape, 1)).astype(BF16)


def dot(a, b):
    return jnp.dot(a, b, preferred_element_type=F32)


def factors_of(sources):
    def apart(i, j):
        part, head = i // GROUP, i % GROUP
        top = (j < HD) & (head == j) & (part < 3)
        return top | ((head == j - HD) & ((part == 3) | (part == 4)))

    pick = zero_one((HD, 2 * HD), apart)
    tops, totals = [], []
    for blocks in sources:
        both = dot(jnp.concatenate([ref[index, :, FEATS:] for ref, index in blocks], axis=0), pick)
        tops.append(both[:, :HD])
        totals.append(both[:, HD:])
    best = functools.reduce(jnp.maximum, tops)
    factors = [jnp.exp2((top - best) * SCALE) for top in tops]
    return best, sum(f * total for f, total in zip(factors, totals)), factors


def spread(factors):
    place = zero_one((2 * HD, FEATS), lambda i, j: i % HD == j // HD)
    return dot(jnp.concatenate(in_parts(factors, 2), axis=1), place)


def sum_into(outs, sources, factors):
    wide = [spread(f) for f in factors]
    for b, (out, index) in enumerate(outs):
        rows = slice(b * ROWS, (b + 1) * ROWS)
        for g in range(GROUP):
            cols = slice(g * HD, (g + 1) * HD)
            terms = [f[rows, cols] * blocks[b][0][blocks[b][1], :, cols].astype(F32) for f, blocks in zip(wide, sources)]
            out[index, :, cols] = sum(terms).astype(BF16)


def merge_into(outs, sources):
    best, total, factors = factors_of(sources)
    join = zero_one((5 * HD, HD), lambda i, j: (i // HD * GROUP + i % HD == j) & (i % HD < GROUP))
    stats = dot(jnp.concatenate([*in_parts(best, 3), *in_parts(total, 2)], axis=1), join).astype(BF16)
    sum_into(outs, sources, factors)
    for b, (out, index) in enumerate(outs):
        out[index, :, FEATS:] = stats[b * ROWS : (b + 1) * ROWS]


def twin_kernel(info, mine, got, *outs):
    z, x, core = info[0], info[1], info[2]
    places, chips = [], []
    for d in range(SIDE):
        for j in range(SIDE):
            places.append((outs[d], j))
            chips.append(jnp.where(core == 0, ((z + d) % SIDE) * SIDE + j, j * SIDE + (x + d) % SIDE))
    merge_into(places, [[(mine, chip) for chip in chips], [(got, chip) for chip in chips]])


def merge_twins(info, mine, got):
    return pl.pallas_call(
        twin_kernel,
        out_shape=[jax.ShapeDtypeStruct((SIDE, ROWS, WIDE), BF16)] * SIDE,
        in_specs=[pl.BlockSpec(memory_space=pltpu.SMEM)] + [whole()] * 2,
        out_specs=[whole()] * SIDE,
        compiler_params=pltpu.CompilerParams(vmem_limit_bytes=24 * MIB),
        name="merge_twins",
    )(info, mine, got)


def four_kernel(*refs):
    merge_into([(refs[-1], j) for j in range(SIDE)], [[(ref, j) for j in range(SIDE)] for ref in refs[:-1]])


def merge_four(parts):
    return pl.pallas_call(
        four_kernel,
        out_shape=jax.ShapeDtypeStruct((SIDE, ROWS, WIDE), BF16),
        in_specs=[whole()] * SIDE,
        out_specs=whole(),
        compiler_params=pltpu.CompilerParams(vmem_limit_bytes=24 * MIB),
        name="merge_four",
    )(*parts)


def final_kernel(*refs):
    sources = [[(ref, j) for j in range(SIDE)] for ref in refs[:-1]]
    _, total, factors = factors_of(sources)
    lane = lax.broadcasted_iota(jnp.int32, total.shape, 1)
    total = jnp.where(lane < GROUP, total, 1.0)
    sum_into([(refs[-1], j) for j in range(SIDE)], sources, [f / total for f in factors])


def merge_final(parts):
    return pl.pallas_call(
        final_kernel,
        out_shape=jax.ShapeDtypeStruct((SIDE, ROWS, FEATS), BF16),
        in_specs=[whole()] * SIDE,
        out_specs=whole(),
        compiler_params=pltpu.CompilerParams(vmem_limit_bytes=24 * MIB),
        name="merge_final",
    )(*parts)


def project_kernel(info, *refs):
    own, other, weight = refs[:SIDE], refs[SIDE : 2 * SIDE], refs[2 * SIDE]
    keep, sends, held = refs[2 * SIDE + 1], refs[2 * SIDE + 2 : 3 * SIDE + 1], refs[-1]
    z, x, core, y = info[0], info[1], info[2], info[3]

    def place(zero, one):
        for d in range(SIDE):
            for j in range(SIDE):
                for half, values, chip in (
                    (0, zero, ((z + d) % SIDE) * SIDE + j),
                    (1, one, j * SIDE + (x + d) % SIDE),
                ):
                    rows = pl.ds(pl.multiple_of(chip * ROWS, ROWS), ROWS)
                    held[rows, half * FEATS : (half + 1) * FEATS] = values[d][j]

    @pl.when(core == 0)
    def _():
        place(own, other)

    @pl.when(core == 1)
    def _():
        place(other, own)

    count = keep.shape[0]
    total = dot(held[...], weight[...])
    for group in range(SIDE):
        rows = total[group * count : (group + 1) * count]
        for d in range(SIDE):

            @pl.when((y + d) % SIDE == group)
            def _(rows=rows, d=d):
                if d == 0:
                    keep[...] = rows
                else:
                    sends[d - 1][...] = rows.astype(BF16)


def project(info, own, other, weight):
    depth, cols = weight.shape
    rows = SIDE * SIDE * ROWS
    return pl.pallas_call(
        project_kernel,
        out_shape=[jax.ShapeDtypeStruct((rows // SIDE, cols), F32)]
        + [jax.ShapeDtypeStruct((rows // SIDE, cols), BF16)] * (SIDE - 1),
        in_specs=[pl.BlockSpec(memory_space=pltpu.SMEM)] + [whole()] * (2 * SIDE + 1),
        out_specs=[whole()] * SIDE,
        scratch_shapes=[pltpu.VMEM((rows, depth), BF16)],
        compiler_params=pltpu.CompilerParams(vmem_limit_bytes=24 * MIB),
        cost_estimate=pl.CostEstimate(flops=2 * rows * depth * cols, bytes_accessed=depth * cols * 2, transcendentals=0),
        name="project",
    )(info, *own, *other, weight)


def on_device(queries, cache, new_kv, lengths, out_weight):
    index = lax.axis_index("ctx")
    z, x, core = index // (2 * SIDE), (index // 2) % SIDE, index % 2
    info = jnp.stack([z, x, core, lax.axis_index("kvh")]).astype(jnp.int32)
    slot = cache.shape[1]
    valid = jnp.clip(lengths - index * slot, 0, slot).astype(jnp.int32)

    request = 2 * z + x // 2
    new = lax.dynamic_slice(new_kv, (request, 0, core, 0), (1, NEW, 1, 2 * HD)).reshape(1, NEW, 2 * HD)
    ahead = split_ahead(cache, None, 0, 1)
    line = stack([queries] + [from_first(queries, s) for s in (1, 2, 3)])
    info, valid, new, line, ahead = lax.optimization_barrier((info, valid, new, line, ahead))
    own = [line] + [from_second(line, s) for s in (1, 2, 3)]
    ahead = split_ahead(cache, ahead, 1, AHEAD - 1)
    *own, ahead = lax.optimization_barrier((*own, ahead))
    other = [from_twin(part) for part in own]

    sent, mine = attend(info, valid, own, other, ahead, cache, new)
    parts = merge_twins(info, mine, from_twin(sent))
    zs = merge_four([parts[0]] + [from_second(parts[SIDE - s], s) for s in (1, 2, 3)])
    rows = merge_final([zs] + [from_first(zs, s) for s in (1, 2, 3)])

    own = [rows] + [from_second(rows, s) for s in (1, 2, 3)]
    other = [from_twin(part) for part in own]
    keep, *sends = project(info, own, other, out_weight)
    total = keep
    for d in (1, 2, 3):
        total = total + from_plane(sends[d - 1], SIDE - d).astype(F32)
    return total.astype(BF16)


def solution(mesh):
    placed = (
        P("ctx", "kvh"),
        P(None, "ctx", "kvh", None),
        P(None, None, "kvh", None),
        P(),
        P("kvh", "ctx"),
    )
    return jax.shard_map(
        on_device, mesh=mesh, in_specs=placed, out_specs=P("kvh", "ctx"), check_vma=False
    )
```

```python
import functools
import math

import jax
import jax.numpy as jnp
from jax import lax
from jax.experimental import pallas as pl
from jax.experimental.pallas import tpu as pltpu
from jax.sharding import PartitionSpec as P

KV_HEADS = 8
QH = 128
HD = 128
REQS = 8
NEW = 32
GROUP = QH // KV_HEADS
AHEAD = 4
SIDE = 4
ROWS = 16
BLOCK = GROUP * ROWS
FEATS = GROUP * HD
WIDE = FEATS + HD
SCALE = HD ** (-0.5) * math.log2(math.e)
EMPTY = -1e30
F32, BF16 = jnp.float32, jnp.bfloat16
MIB = 2**20


def at(z, x, core):
    return ((z % SIDE) * SIDE + x % SIDE) * 2 + core


def places():
    return [(z, x, c) for z in range(SIDE) for x in range(SIDE) for c in range(2)]


def from_first(value, step):
    pairs = [(at(z, x + step, c) if c == 0 else at(z + step, x, c), at(z, x, c)) for z, x, c in places()]
    return lax.ppermute(value, "ctx", pairs)


def from_second(value, step):
    pairs = [(at(z + step, x, c) if c == 0 else at(z, x + step, c), at(z, x, c)) for z, x, c in places()]
    return lax.ppermute(value, "ctx", pairs)


def from_twin(value):
    return lax.ppermute(value, "ctx", [(at(z, x, 1 - c), at(z, x, c)) for z, x, c in places()])


def from_plane(value, step):
    return lax.ppermute(value, "kvh", [((s + step) % SIDE, s) for s in range(SIDE)])


def whole():
    return pl.BlockSpec(memory_space=pltpu.VMEM)


def stack_kernel(*refs):
    for i, ref in enumerate(refs[:-1]):
        refs[-1][i] = ref[...]


def stack(parts):
    return pl.pallas_call(
        stack_kernel,
        out_shape=jax.ShapeDtypeStruct((len(parts), *parts[0].shape), parts[0].dtype),
        in_specs=[whole()] * len(parts),
        out_specs=whole(),
        compiler_params=pltpu.CompilerParams(vmem_limit_bytes=8 * MIB),
        name="stack",
    )(*parts)


def dot_nt(a, b):
    return lax.dot_general(a, b, (((1,), (1,)), ((), ())), preferred_element_type=F32)


def weigh(s):
    top = jnp.max(s, axis=1, keepdims=True)
    return top, jnp.exp2((s - top) * SCALE).astype(BF16)


def sum_up(w, values):
    ones = jnp.ones(values.shape, BF16)
    both = jnp.dot(w, jnp.concatenate([values, ones], axis=1), preferred_element_type=F32)
    return both[:, :HD], both[:, HD:]


def in_parts(value, count):
    parts = []
    for _ in range(count):
        part = value.astype(BF16)
        parts.append(part)
        value = value - part.astype(F32)
    return parts


def pack_stats(top, total):
    rest = jnp.zeros((ROWS, HD - 5 * GROUP), BF16)
    return jnp.concatenate([*in_parts(top, 3), *in_parts(total, 2), rest], axis=1)


def put_partial(out, index, top, summed, total):
    lane = lax.broadcasted_iota(jnp.int32, (ROWS, HD), 1)
    tops = totals = jnp.zeros((ROWS, HD), F32)
    for g in range(GROUP):
        rows = slice(g * ROWS, (g + 1) * ROWS)
        out[index, :, g * HD : (g + 1) * HD] = summed[rows].astype(BF16)
        tops = jnp.where(lane == g, top[rows], tops)
        totals = jnp.where(lane == g, total[rows], totals)
    out[index, :, FEATS:] = pack_stats(tops[:, :GROUP], totals[:, :GROUP])


def assemble(info, own, other, held):
    z, x, core = info[0], info[1], info[2]
    for dz in range(SIDE):
        plane = (z + dz) % SIDE

        def lay(zeros, ones, dz=dz, plane=plane):
            for dx in range(SIDE):
                zero, one = zeros(dz, dx), ones(dz, dx)
                for head in range(2):
                    for g in range(GROUP):
                        cols = slice(head * FEATS + g * HD, head * FEATS + (g + 1) * HD)
                        pair = jnp.concatenate([zero[:, cols].astype(F32), one[:, cols].astype(F32)], axis=0)
                        held[head, plane * SIDE + (x + dx) % SIDE, g * ROWS : (g + 1) * ROWS, :] = pair.astype(BF16)

        @pl.when(core == 0)
        def _(lay=lay):
            lay(lambda dz, dx: own[dz][dx], lambda dz, dx: other[dx][dz])

        @pl.when(core == 1)
        def _(lay=lay):
            lay(lambda dz, dx: other[dz][dx], lambda dz, dx: own[dx][dz])


def split_heads(cache, at, out):
    r = lax.broadcasted_iota(jnp.int32, (2 * HD, 2 * HD), 0)
    c = lax.broadcasted_iota(jnp.int32, (2 * HD, 2 * HD), 1)
    pick = (c == jnp.where(r < HD, 2 * r, 2 * (r - HD) + 1)).astype(BF16)
    for i in range(cache.shape[1] // HD):
        rows = slice(i * HD, (i + 1) * HD)
        both = cache[at, rows].reshape(2 * HD, 2 * HD)
        apart = jnp.dot(pick, both, preferred_element_type=F32).astype(BF16)
        out(0, rows, apart[:HD])
        out(1, rows, apart[HD:])


def ahead_kernel(cache, *refs):
    out = refs[-1]

    def put(head, rows, value):
        out[0, head, rows] = value

    split_heads(cache, 0, put)


def split_ahead(cache, held, begin, count):
    per = cache.shape[1]
    return pl.pallas_call(
        ahead_kernel,
        grid=(count,),
        in_specs=[pl.BlockSpec((1, per, 2, 2 * HD), lambda i: (begin + i, 0, 0, 0))]
        + ([] if held is None else [pl.BlockSpec(memory_space=pl.ANY)]),
        out_specs=pl.BlockSpec((1, 2, per, 2 * HD), lambda i: (begin + i, 0, 0, 0)),
        out_shape=jax.ShapeDtypeStruct((AHEAD, 2, per, 2 * HD), BF16),
        input_output_aliases={} if held is None else {1: 0},
        compiler_params=pltpu.CompilerParams(vmem_limit_bytes=54 * MIB),
        cost_estimate=pl.CostEstimate(flops=0, bytes_accessed=count * 8 * MIB, transcendentals=0),
        name="split_ahead",
    )(cache, *([] if held is None else [held]))


def attend_kernel(info, valid, *refs):
    own, other, ahead, cache, new = refs[:SIDE], refs[SIDE : 2 * SIDE], *refs[2 * SIDE : 2 * SIDE + 3]
    sent, mine, queries, keys, held, mine_new, arrived = refs[2 * SIDE + 3 :]
    step = pl.program_id(0)
    core = info[2]
    slot = cache.shape[1]
    side = step % 2

    def fetch(request):
        if request < AHEAD:
            return pltpu.make_async_copy(
                ahead.at[request], keys.at[request // 2 % 2, request % 2], arrived.at[request]
            )
        return pltpu.make_async_copy(cache.at[request], held.at[request - AHEAD], arrived.at[request])

    @pl.when(step == 0)
    def _():
        for request in range(2):
            fetch(request).start()
        assemble(info, own, other, queries)

    for now in range(REQS // 2):

        @pl.when(step == now)
        def _(now=now):
            for r in range(2):
                fetch(2 * now + r).wait()
            if now == 0:
                for request in range(2, REQS):
                    fetch(request).start()

    for r in range(2):

        @pl.when(2 * step + r >= AHEAD)
        def _(r=r):
            def put(head, rows, value):
                keys[side, r, head, rows] = value

            split_heads(held, 2 * step + r - AHEAD, put)

    first, second = valid[2 * step], valid[2 * step + 1]
    where = [
        (r, head, out, half)
        for r in range(2)
        for head, out in ((1 - core, sent), (core, mine))
        for half in range(2)
    ]

    def scores(r, head, _, half):
        return dot_nt(queries[head, 4 * step + 2 * r + half], keys[side, r, head, :, :HD])

    def finish(r, head, out, half, s):
        top, w = weigh(s)
        put_partial(out, 2 * r + half, top, *sum_up(w, keys[side, r, head, :, HD:]))

    full = jnp.logical_and(first >= slot, second >= slot)
    empty = jnp.logical_and(first <= 0, second <= 0)

    def run(biases):
        def masked(block):
            s = scores(*block)
            return s if biases is None else s + biases[block[0]]

        s = masked(where[0])
        for i, block in enumerate(where):
            later = masked(where[i + 1]) if i + 1 < len(where) else None
            finish(*block, s)
            s = later

    @pl.when(full)
    def _():
        run(None)

    @pl.when(jnp.logical_not(jnp.logical_or(full, empty)))
    def _():
        position = lax.broadcasted_iota(jnp.int32, (1, slot), 1)
        run([jnp.where(position < count, 0.0, EMPTY) for count in (first, second)])

    @pl.when(empty)
    def _():
        none = pack_stats(jnp.full((ROWS, GROUP), EMPTY, F32), jnp.zeros((ROWS, GROUP), F32))
        for out in (sent, mine):
            for i in range(out.shape[0]):
                out[i, :, :FEATS] = jnp.zeros((ROWS, FEATS), BF16)
                out[i, :, FEATS:] = none

    z, x = info[0], info[1]

    @pl.when(step == z)
    def _():
        s = dot_nt(queries[core, z * SIDE + x], new[0, :, :HD])
        token = (x % 2) * ROWS + lax.broadcasted_iota(jnp.int32, s.shape, 0) % ROWS
        key = lax.broadcasted_iota(jnp.int32, s.shape, 1)
        top, w = weigh(jnp.where(key <= token, s, EMPTY))
        put_partial(mine_new, 0, top, *sum_up(w, new[0, :, HD:]))
        merge_into([(mine, x)], [[(mine, x)], [(mine_new, 0)]])


def attend(info, valid, own, other, ahead, cache, new):
    reqs, per = cache.shape[:2]
    blocks = jax.ShapeDtypeStruct((2 * reqs, ROWS, WIDE), BF16)
    return pl.pallas_call(
        attend_kernel,
        out_shape=[blocks, blocks],
        grid_spec=pltpu.PrefetchScalarGridSpec(
            num_scalar_prefetch=2,
            grid=(reqs // 2,),
            in_specs=[whole()] * (2 * SIDE) + [pl.BlockSpec(memory_space=pl.ANY)] * 2 + [whole()],
            out_specs=[pl.BlockSpec((4, ROWS, WIDE), lambda i, info, valid: (i, 0, 0))] * 2,
            scratch_shapes=[
                pltpu.VMEM((2, SIDE * SIDE, BLOCK, HD), BF16),
                pltpu.VMEM((2, 2, 2, per, 2 * HD), BF16),
                pltpu.VMEM((REQS - AHEAD, *cache.shape[1:]), BF16),
                pltpu.VMEM((1, ROWS, WIDE), BF16),
                pltpu.SemaphoreType.DMA((REQS,)),
            ],
        ),
        compiler_params=pltpu.CompilerParams(vmem_limit_bytes=46 * MIB),
        cost_estimate=pl.CostEstimate(
            flops=16 * reqs * BLOCK * per * HD, bytes_accessed=reqs * per * 4 * HD * 2, transcendentals=0
        ),
        name="attend",
    )(info, valid, *own, *other, ahead, cache, new)


def zero_one(shape, test):
    return test(lax.broadcasted_iota(jnp.int32, shape, 0), lax.broadcasted_iota(jnp.int32, shape, 1)).astype(BF16)


def dot(a, b):
    return jnp.dot(a, b, preferred_element_type=F32)


def factors_of(sources):
    def apart(i, j):
        part, head = i // GROUP, i % GROUP
        top = (j < HD) & (head == j) & (part < 3)
        return top | ((head == j - HD) & ((part == 3) | (part == 4)))

    pick = zero_one((HD, 2 * HD), apart)
    tops, totals = [], []
    for blocks in sources:
        both = dot(jnp.concatenate([ref[index, :, FEATS:] for ref, index in blocks], axis=0), pick)
        tops.append(both[:, :HD])
        totals.append(both[:, HD:])
    best = functools.reduce(jnp.maximum, tops)
    factors = [jnp.exp2((top - best) * SCALE) for top in tops]
    return best, sum(f * total for f, total in zip(factors, totals)), factors


def spread(factors):
    place = zero_one((2 * HD, FEATS), lambda i, j: i % HD == j // HD)
    return dot(jnp.concatenate(in_parts(factors, 2), axis=1), place)


def sum_into(outs, sources, factors):
    wide = [spread(f) for f in factors]
    for b, (out, index) in enumerate(outs):
        rows = slice(b * ROWS, (b + 1) * ROWS)
        for g in range(GROUP):
            cols = slice(g * HD, (g + 1) * HD)
            terms = [f[rows, cols] * blocks[b][0][blocks[b][1], :, cols].astype(F32) for f, blocks in zip(wide, sources)]
            out[index, :, cols] = sum(terms).astype(BF16)


def merge_into(outs, sources):
    best, total, factors = factors_of(sources)
    join = zero_one((5 * HD, HD), lambda i, j: (i // HD * GROUP + i % HD == j) & (i % HD < GROUP))
    stats = dot(jnp.concatenate([*in_parts(best, 3), *in_parts(total, 2)], axis=1), join).astype(BF16)
    sum_into(outs, sources, factors)
    for b, (out, index) in enumerate(outs):
        out[index, :, FEATS:] = stats[b * ROWS : (b + 1) * ROWS]


def twin_kernel(info, mine, got, *outs):
    z, x, core = info[0], info[1], info[2]
    places, chips = [], []
    for d in range(SIDE):
        for j in range(SIDE):
            places.append((outs[d], j))
            chips.append(jnp.where(core == 0, ((z + d) % SIDE) * SIDE + j, j * SIDE + (x + d) % SIDE))
    merge_into(places, [[(mine, chip) for chip in chips], [(got, chip) for chip in chips]])


def merge_twins(info, mine, got):
    return pl.pallas_call(
        twin_kernel,
        out_shape=[jax.ShapeDtypeStruct((SIDE, ROWS, WIDE), BF16)] * SIDE,
        in_specs=[pl.BlockSpec(memory_space=pltpu.SMEM)] + [whole()] * 2,
        out_specs=[whole()] * SIDE,
        compiler_params=pltpu.CompilerParams(vmem_limit_bytes=24 * MIB),
        name="merge_twins",
    )(info, mine, got)


def four_kernel(*refs):
    merge_into([(refs[-1], j) for j in range(SIDE)], [[(ref, j) for j in range(SIDE)] for ref in refs[:-1]])


def merge_four(parts):
    return pl.pallas_call(
        four_kernel,
        out_shape=jax.ShapeDtypeStruct((SIDE, ROWS, WIDE), BF16),
        in_specs=[whole()] * SIDE,
        out_specs=whole(),
        compiler_params=pltpu.CompilerParams(vmem_limit_bytes=24 * MIB),
        name="merge_four",
    )(*parts)


def final_kernel(*refs):
    sources = [[(ref, j) for j in range(SIDE)] for ref in refs[:-1]]
    _, total, factors = factors_of(sources)
    lane = lax.broadcasted_iota(jnp.int32, total.shape, 1)
    total = jnp.where(lane < GROUP, total, 1.0)
    sum_into([(refs[-1], j) for j in range(SIDE)], sources, [f / total for f in factors])


def merge_final(parts):
    return pl.pallas_call(
        final_kernel,
        out_shape=jax.ShapeDtypeStruct((SIDE, ROWS, FEATS), BF16),
        in_specs=[whole()] * SIDE,
        out_specs=whole(),
        compiler_params=pltpu.CompilerParams(vmem_limit_bytes=24 * MIB),
        name="merge_final",
    )(*parts)


def project_kernel(info, *refs):
    own, other, weight = refs[:SIDE], refs[SIDE : 2 * SIDE], refs[2 * SIDE]
    keep, sends, held = refs[2 * SIDE + 1], refs[2 * SIDE + 2 : 3 * SIDE + 1], refs[-1]
    z, x, core, y = info[0], info[1], info[2], info[3]

    def place(zero, one):
        for d in range(SIDE):
            for j in range(SIDE):
                for half, values, chip in (
                    (0, zero, ((z + d) % SIDE) * SIDE + j),
                    (1, one, j * SIDE + (x + d) % SIDE),
                ):
                    rows = pl.ds(pl.multiple_of(chip * ROWS, ROWS), ROWS)
                    held[rows, half * FEATS : (half + 1) * FEATS] = values[d][j]

    @pl.when(core == 0)
    def _():
        place(own, other)

    @pl.when(core == 1)
    def _():
        place(other, own)

    count = keep.shape[0]
    total = dot(held[...], weight[...])
    for group in range(SIDE):
        rows = total[group * count : (group + 1) * count]
        for d in range(SIDE):

            @pl.when((y + d) % SIDE == group)
            def _(rows=rows, d=d):
                if d == 0:
                    keep[...] = rows
                else:
                    sends[d - 1][...] = rows.astype(BF16)


def project(info, own, other, weight):
    depth, cols = weight.shape
    rows = SIDE * SIDE * ROWS
    return pl.pallas_call(
        project_kernel,
        out_shape=[jax.ShapeDtypeStruct((rows // SIDE, cols), F32)]
        + [jax.ShapeDtypeStruct((rows // SIDE, cols), BF16)] * (SIDE - 1),
        in_specs=[pl.BlockSpec(memory_space=pltpu.SMEM)] + [whole()] * (2 * SIDE + 1),
        out_specs=[whole()] * SIDE,
        scratch_shapes=[pltpu.VMEM((rows, depth), BF16)],
        compiler_params=pltpu.CompilerParams(vmem_limit_bytes=24 * MIB),
        cost_estimate=pl.CostEstimate(flops=2 * rows * depth * cols, bytes_accessed=depth * cols * 2, transcendentals=0),
        name="project",
    )(info, *own, *other, weight)


def on_device(queries, cache, new_kv, lengths, out_weight):
    index = lax.axis_index("ctx")
    z, x, core = index // (2 * SIDE), (index // 2) % SIDE, index % 2
    info = jnp.stack([z, x, core, lax.axis_index("kvh")]).astype(jnp.int32)
    slot = cache.shape[1]
    valid = jnp.clip(lengths - index * slot, 0, slot).astype(jnp.int32)

    request = 2 * z + x // 2
    new = lax.dynamic_slice(new_kv, (request, 0, core, 0), (1, NEW, 1, 2 * HD)).reshape(1, NEW, 2 * HD)
    ahead = split_ahead(cache, None, 0, 1)
    line = stack([queries] + [from_first(queries, s) for s in (1, 2, 3)])
    info, valid, new, line, ahead = lax.optimization_barrier((info, valid, new, line, ahead))
    own = [line] + [from_second(line, s) for s in (1, 2, 3)]
    ahead = split_ahead(cache, ahead, 1, AHEAD - 1)
    *own, ahead = lax.optimization_barrier((*own, ahead))
    other = [from_twin(part) for part in own]

    sent, mine = attend(info, valid, own, other, ahead, cache, new)
    parts = merge_twins(info, mine, from_twin(sent))
    zs = merge_four([parts[0]] + [from_second(parts[SIDE - s], s) for s in (1, 2, 3)])
    rows = merge_final([zs] + [from_first(zs, s) for s in (1, 2, 3)])

    own = [rows] + [from_second(rows, s) for s in (1, 2, 3)]
    other = [from_twin(part) for part in own]
    keep, *sends = project(info, own, other, out_weight)
    total = keep
    for d in (1, 2, 3):
        total = total + from_plane(sends[d - 1], SIDE - d).astype(F32)
    return total.astype(BF16)


def solution(mesh):
    placed = (
        P("ctx", "kvh"),
        P(None, "ctx", "kvh", None),
        P(None, None, "kvh", None),
        P(),
        P("kvh", "ctx"),
    )
    return jax.shard_map(
        on_device, mesh=mesh, in_specs=placed, out_specs=P("kvh", "ctx"), check_vma=False
    )
```

```python
import functools
import math

import jax
import jax.numpy as jnp
from jax import lax
from jax.experimental import pallas as pl
from jax.experimental.pallas import tpu as pltpu
from jax.sharding import PartitionSpec as P

KV_HEADS = 8
QH = 128
HD = 128
REQS = 8
NEW = 32
GROUP = QH // KV_HEADS
AHEAD = 4
SIDE = 4
ROWS = 16
BLOCK = GROUP * ROWS
FEATS = GROUP * HD
WIDE = FEATS + HD
SCALE = HD ** (-0.5) * math.log2(math.e)
EMPTY = -1e30
F32, BF16 = jnp.float32, jnp.bfloat16
MIB = 2**20


def at(z, x, core):
    return ((z % SIDE) * SIDE + x % SIDE) * 2 + core


def places():
    return [(z, x, c) for z in range(SIDE) for x in range(SIDE) for c in range(2)]


def from_first(value, step):
    pairs = [(at(z, x + step, c) if c == 0 else at(z + step, x, c), at(z, x, c)) for z, x, c in places()]
    return lax.ppermute(value, "ctx", pairs)


def from_second(value, step):
    pairs = [(at(z + step, x, c) if c == 0 else at(z, x + step, c), at(z, x, c)) for z, x, c in places()]
    return lax.ppermute(value, "ctx", pairs)


def from_twin(value):
    return lax.ppermute(value, "ctx", [(at(z, x, 1 - c), at(z, x, c)) for z, x, c in places()])


def from_plane(value, step):
    return lax.ppermute(value, "kvh", [((s + step) % SIDE, s) for s in range(SIDE)])


def whole():
    return pl.BlockSpec(memory_space=pltpu.VMEM)


def stack_kernel(*refs):
    for i, ref in enumerate(refs[:-1]):
        refs[-1][i] = ref[...]


def stack(parts):
    return pl.pallas_call(
        stack_kernel,
        out_shape=jax.ShapeDtypeStruct((len(parts), *parts[0].shape), parts[0].dtype),
        in_specs=[whole()] * len(parts),
        out_specs=whole(),
        compiler_params=pltpu.CompilerParams(vmem_limit_bytes=8 * MIB),
        name="stack",
    )(*parts)


def from_all(move, value_for):
    got = {step: move(value_for(step), step) for step in (2, 1, 3)}
    return [got[step] for step in (1, 2, 3)]


def dot_nt(a, b):
    return lax.dot_general(a, b, (((1,), (1,)), ((), ())), preferred_element_type=F32)


def weigh(s):
    top = jnp.max(s, axis=1, keepdims=True)
    return top, jnp.exp2((s - top) * SCALE).astype(BF16)


def sum_up(w, values):
    ones = jnp.ones(values.shape, BF16)
    both = jnp.dot(w, jnp.concatenate([values, ones], axis=1), preferred_element_type=F32)
    return both[:, :HD], both[:, HD:]


def in_parts(value, count):
    parts = []
    for _ in range(count):
        part = value.astype(BF16)
        parts.append(part)
        value = value - part.astype(F32)
    return parts


def pack_stats(top, total):
    rest = jnp.zeros((ROWS, HD - 5 * GROUP), BF16)
    return jnp.concatenate([*in_parts(top, 3), *in_parts(total, 2), rest], axis=1)


def put_partial(out, index, top, summed, total):
    lane = lax.broadcasted_iota(jnp.int32, (ROWS, HD), 1)
    tops = totals = jnp.zeros((ROWS, HD), F32)
    for g in range(GROUP):
        rows = slice(g * ROWS, (g + 1) * ROWS)
        out[index, :, g * HD : (g + 1) * HD] = summed[rows].astype(BF16)
        tops = jnp.where(lane == g, top[rows], tops)
        totals = jnp.where(lane == g, total[rows], totals)
    out[index, :, FEATS:] = pack_stats(tops[:, :GROUP], totals[:, :GROUP])


def assemble(info, own, other, held):
    z, x, core = info[0], info[1], info[2]
    for dz in range(SIDE):
        plane = (z + dz) % SIDE

        def lay(zeros, ones, dz=dz, plane=plane):
            for dx in range(SIDE):
                zero, one = zeros(dz, dx), ones(dz, dx)
                for head in range(2):
                    for g in range(GROUP):
                        cols = slice(head * FEATS + g * HD, head * FEATS + (g + 1) * HD)
                        pair = jnp.concatenate([zero[:, cols].astype(F32), one[:, cols].astype(F32)], axis=0)
                        held[head, plane * SIDE + (x + dx) % SIDE, g * ROWS : (g + 1) * ROWS, :] = pair.astype(BF16)

        @pl.when(core == 0)
        def _(lay=lay):
            lay(lambda dz, dx: own[dz][dx], lambda dz, dx: other[dx][dz])

        @pl.when(core == 1)
        def _(lay=lay):
            lay(lambda dz, dx: other[dz][dx], lambda dz, dx: own[dx][dz])


def split_heads(cache, at, out):
    r = lax.broadcasted_iota(jnp.int32, (2 * HD, 2 * HD), 0)
    c = lax.broadcasted_iota(jnp.int32, (2 * HD, 2 * HD), 1)
    pick = (c == jnp.where(r < HD, 2 * r, 2 * (r - HD) + 1)).astype(BF16)
    for i in range(cache.shape[1] // HD):
        rows = slice(i * HD, (i + 1) * HD)
        both = cache[at, rows].reshape(2 * HD, 2 * HD)
        apart = jnp.dot(pick, both, preferred_element_type=F32).astype(BF16)
        out(0, rows, apart[:HD])
        out(1, rows, apart[HD:])


def ahead_kernel(cache, *refs):
    out = refs[-1]

    def put(head, rows, value):
        out[0, head, rows] = value

    split_heads(cache, 0, put)


def split_ahead(cache, held, begin, count):
    per = cache.shape[1]
    return pl.pallas_call(
        ahead_kernel,
        grid=(count,),
        in_specs=[pl.BlockSpec((1, per, 2, 2 * HD), lambda i: (begin + i, 0, 0, 0))]
        + ([] if held is None else [pl.BlockSpec(memory_space=pl.ANY)]),
        out_specs=pl.BlockSpec((1, 2, per, 2 * HD), lambda i: (begin + i, 0, 0, 0)),
        out_shape=jax.ShapeDtypeStruct((AHEAD, 2, per, 2 * HD), BF16),
        input_output_aliases={} if held is None else {1: 0},
        compiler_params=pltpu.CompilerParams(vmem_limit_bytes=54 * MIB),
        cost_estimate=pl.CostEstimate(flops=0, bytes_accessed=count * 8 * MIB, transcendentals=0),
        name="split_ahead",
    )(cache, *([] if held is None else [held]))


def attend_kernel(info, valid, *refs):
    own, other, ahead, cache, new = refs[:SIDE], refs[SIDE : 2 * SIDE], *refs[2 * SIDE : 2 * SIDE + 3]
    sent, mine, queries, keys, held, mine_new, arrived = refs[2 * SIDE + 3 :]
    step = pl.program_id(0)
    core = info[2]
    slot = cache.shape[1]
    side = step % 2

    def fetch(request):
        if request < AHEAD:
            return pltpu.make_async_copy(
                ahead.at[request], keys.at[request // 2 % 2, request % 2], arrived.at[request]
            )
        return pltpu.make_async_copy(cache.at[request], held.at[request - AHEAD], arrived.at[request])

    @pl.when(step == 0)
    def _():
        for request in range(2):
            fetch(request).start()
        assemble(info, own, other, queries)

    for now in range(REQS // 2):

        @pl.when(step == now)
        def _(now=now):
            for r in range(2):
                fetch(2 * now + r).wait()
            if now == 0:
                for request in range(2, REQS):
                    fetch(request).start()

    for r in range(2):

        @pl.when(2 * step + r >= AHEAD)
        def _(r=r):
            def put(head, rows, value):
                keys[side, r, head, rows] = value

            split_heads(held, 2 * step + r - AHEAD, put)

    first, second = valid[2 * step], valid[2 * step + 1]
    where = [
        (r, head, out, half)
        for r in range(2)
        for head, out in ((1 - core, sent), (core, mine))
        for half in range(2)
    ]

    def scores(r, head, _, half):
        return dot_nt(queries[head, 4 * step + 2 * r + half], keys[side, r, head, :, :HD])

    def finish(r, head, out, half, s):
        top, w = weigh(s)
        put_partial(out, 2 * r + half, top, *sum_up(w, keys[side, r, head, :, HD:]))

    full = jnp.logical_and(first >= slot, second >= slot)
    empty = jnp.logical_and(first <= 0, second <= 0)

    def run(biases):
        def masked(block):
            s = scores(*block)
            return s if biases is None else s + biases[block[0]]

        s = masked(where[0])
        for i, block in enumerate(where):
            later = masked(where[i + 1]) if i + 1 < len(where) else None
            finish(*block, s)
            s = later

    @pl.when(full)
    def _():
        run(None)

    @pl.when(jnp.logical_not(jnp.logical_or(full, empty)))
    def _():
        position = lax.broadcasted_iota(jnp.int32, (1, slot), 1)
        run([jnp.where(position < count, 0.0, EMPTY) for count in (first, second)])

    @pl.when(empty)
    def _():
        none = pack_stats(jnp.full((ROWS, GROUP), EMPTY, F32), jnp.zeros((ROWS, GROUP), F32))
        for out in (sent, mine):
            for i in range(out.shape[0]):
                out[i, :, :FEATS] = jnp.zeros((ROWS, FEATS), BF16)
                out[i, :, FEATS:] = none

    z, x = info[0], info[1]

    @pl.when(step == z)
    def _():
        s = dot_nt(queries[core, z * SIDE + x], new[0, :, :HD])
        token = (x % 2) * ROWS + lax.broadcasted_iota(jnp.int32, s.shape, 0) % ROWS
        key = lax.broadcasted_iota(jnp.int32, s.shape, 1)
        top, w = weigh(jnp.where(key <= token, s, EMPTY))
        put_partial(mine_new, 0, top, *sum_up(w, new[0, :, HD:]))
        merge_into([(mine, x)], [[(mine, x)], [(mine_new, 0)]])


def attend(info, valid, own, other, ahead, cache, new):
    reqs, per = cache.shape[:2]
    blocks = jax.ShapeDtypeStruct((2 * reqs, ROWS, WIDE), BF16)
    return pl.pallas_call(
        attend_kernel,
        out_shape=[blocks, blocks],
        grid_spec=pltpu.PrefetchScalarGridSpec(
            num_scalar_prefetch=2,
            grid=(reqs // 2,),
            in_specs=[whole()] * (2 * SIDE) + [pl.BlockSpec(memory_space=pl.ANY)] * 2 + [whole()],
            out_specs=[pl.BlockSpec((4, ROWS, WIDE), lambda i, info, valid: (i, 0, 0))] * 2,
            scratch_shapes=[
                pltpu.VMEM((2, SIDE * SIDE, BLOCK, HD), BF16),
                pltpu.VMEM((2, 2, 2, per, 2 * HD), BF16),
                pltpu.VMEM((REQS - AHEAD, *cache.shape[1:]), BF16),
                pltpu.VMEM((1, ROWS, WIDE), BF16),
                pltpu.SemaphoreType.DMA((REQS,)),
            ],
        ),
        compiler_params=pltpu.CompilerParams(vmem_limit_bytes=46 * MIB),
        cost_estimate=pl.CostEstimate(
            flops=16 * reqs * BLOCK * per * HD, bytes_accessed=reqs * per * 4 * HD * 2, transcendentals=0
        ),
        name="attend",
    )(info, valid, *own, *other, ahead, cache, new)


def zero_one(shape, test):
    return test(lax.broadcasted_iota(jnp.int32, shape, 0), lax.broadcasted_iota(jnp.int32, shape, 1)).astype(BF16)


def dot(a, b):
    return jnp.dot(a, b, preferred_element_type=F32)


def factors_of(sources):
    def apart(i, j):
        part, head = i // GROUP, i % GROUP
        top = (j < HD) & (head == j) & (part < 3)
        return top | ((head == j - HD) & ((part == 3) | (part == 4)))

    pick = zero_one((HD, 2 * HD), apart)
    tops, totals = [], []
    for blocks in sources:
        both = dot(jnp.concatenate([ref[index, :, FEATS:] for ref, index in blocks], axis=0), pick)
        tops.append(both[:, :HD])
        totals.append(both[:, HD:])
    best = functools.reduce(jnp.maximum, tops)
    factors = [jnp.exp2((top - best) * SCALE) for top in tops]
    return best, sum(f * total for f, total in zip(factors, totals)), factors


def spread(factors):
    place = zero_one((2 * HD, FEATS), lambda i, j: i % HD == j // HD)
    return dot(jnp.concatenate(in_parts(factors, 2), axis=1), place)


def sum_into(outs, sources, factors):
    wide = [spread(f) for f in factors]
    for b, (out, index) in enumerate(outs):
        rows = slice(b * ROWS, (b + 1) * ROWS)
        for g in range(GROUP):
            cols = slice(g * HD, (g + 1) * HD)
            terms = [f[rows, cols] * blocks[b][0][blocks[b][1], :, cols].astype(F32) for f, blocks in zip(wide, sources)]
            out[index, :, cols] = sum(terms).astype(BF16)


def merge_into(outs, sources):
    best, total, factors = factors_of(sources)
    join = zero_one((5 * HD, HD), lambda i, j: (i // HD * GROUP + i % HD == j) & (i % HD < GROUP))
    stats = dot(jnp.concatenate([*in_parts(best, 3), *in_parts(total, 2)], axis=1), join).astype(BF16)
    sum_into(outs, sources, factors)
    for b, (out, index) in enumerate(outs):
        out[index, :, FEATS:] = stats[b * ROWS : (b + 1) * ROWS]


def twin_kernel(info, mine, got, *outs):
    z, x, core = info[0], info[1], info[2]
    places, chips = [], []
    for d in range(SIDE):
        for j in range(SIDE):
            places.append((outs[d], j))
            chips.append(jnp.where(core == 0, ((z + d) % SIDE) * SIDE + j, j * SIDE + (x + d) % SIDE))
    merge_into(places, [[(mine, chip) for chip in chips], [(got, chip) for chip in chips]])


def merge_twins(info, mine, got):
    return pl.pallas_call(
        twin_kernel,
        out_shape=[jax.ShapeDtypeStruct((SIDE, ROWS, WIDE), BF16)] * SIDE,
        in_specs=[pl.BlockSpec(memory_space=pltpu.SMEM)] + [whole()] * 2,
        out_specs=[whole()] * SIDE,
        compiler_params=pltpu.CompilerParams(vmem_limit_bytes=24 * MIB),
        name="merge_twins",
    )(info, mine, got)


def four_kernel(*refs):
    merge_into([(refs[-1], j) for j in range(SIDE)], [[(ref, j) for j in range(SIDE)] for ref in refs[:-1]])


def merge_four(parts):
    return pl.pallas_call(
        four_kernel,
        out_shape=jax.ShapeDtypeStruct((SIDE, ROWS, WIDE), BF16),
        in_specs=[whole()] * SIDE,
        out_specs=whole(),
        compiler_params=pltpu.CompilerParams(vmem_limit_bytes=24 * MIB),
        name="merge_four",
    )(*parts)


def final_kernel(*refs):
    sources = [[(ref, j) for j in range(SIDE)] for ref in refs[:-1]]
    _, total, factors = factors_of(sources)
    lane = lax.broadcasted_iota(jnp.int32, total.shape, 1)
    total = jnp.where(lane < GROUP, total, 1.0)
    sum_into([(refs[-1], j) for j in range(SIDE)], sources, [f / total for f in factors])


def merge_final(parts):
    return pl.pallas_call(
        final_kernel,
        out_shape=jax.ShapeDtypeStruct((SIDE, ROWS, FEATS), BF16),
        in_specs=[whole()] * SIDE,
        out_specs=whole(),
        compiler_params=pltpu.CompilerParams(vmem_limit_bytes=24 * MIB),
        name="merge_final",
    )(*parts)


def project_kernel(info, *refs):
    own, other, weight = refs[:SIDE], refs[SIDE : 2 * SIDE], refs[2 * SIDE]
    keep, sends, held = refs[2 * SIDE + 1], refs[2 * SIDE + 2 : 3 * SIDE + 1], refs[-1]
    z, x, core, y = info[0], info[1], info[2], info[3]

    def place(zero, one):
        for d in range(SIDE):
            for j in range(SIDE):
                for half, values, chip in (
                    (0, zero, ((z + d) % SIDE) * SIDE + j),
                    (1, one, j * SIDE + (x + d) % SIDE),
                ):
                    rows = pl.ds(pl.multiple_of(chip * ROWS, ROWS), ROWS)
                    held[rows, half * FEATS : (half + 1) * FEATS] = values[d][j]

    @pl.when(core == 0)
    def _():
        place(own, other)

    @pl.when(core == 1)
    def _():
        place(other, own)

    count = keep.shape[0]
    total = dot(held[...], weight[...])
    for group in range(SIDE):
        rows = total[group * count : (group + 1) * count]
        for d in range(SIDE):

            @pl.when((y + d) % SIDE == group)
            def _(rows=rows, d=d):
                if d == 0:
                    keep[...] = rows
                else:
                    sends[d - 1][...] = rows.astype(BF16)


def project(info, own, other, weight):
    depth, cols = weight.shape
    rows = SIDE * SIDE * ROWS
    return pl.pallas_call(
        project_kernel,
        out_shape=[jax.ShapeDtypeStruct((rows // SIDE, cols), F32)]
        + [jax.ShapeDtypeStruct((rows // SIDE, cols), BF16)] * (SIDE - 1),
        in_specs=[pl.BlockSpec(memory_space=pltpu.SMEM)] + [whole()] * (2 * SIDE + 1),
        out_specs=[whole()] * SIDE,
        scratch_shapes=[pltpu.VMEM((rows, depth), BF16)],
        compiler_params=pltpu.CompilerParams(vmem_limit_bytes=24 * MIB),
        cost_estimate=pl.CostEstimate(flops=2 * rows * depth * cols, bytes_accessed=depth * cols * 2, transcendentals=0),
        name="project",
    )(info, *own, *other, weight)


def on_device(queries, cache, new_kv, lengths, out_weight):
    index = lax.axis_index("ctx")
    z, x, core = index // (2 * SIDE), (index // 2) % SIDE, index % 2
    info = jnp.stack([z, x, core, lax.axis_index("kvh")]).astype(jnp.int32)
    slot = cache.shape[1]
    valid = jnp.clip(lengths - index * slot, 0, slot).astype(jnp.int32)

    request = 2 * z + x // 2
    new = lax.dynamic_slice(new_kv, (request, 0, core, 0), (1, NEW, 1, 2 * HD)).reshape(1, NEW, 2 * HD)
    ahead = split_ahead(cache, None, 0, 1)
    line = stack([queries] + from_all(from_first, lambda _: queries))
    info, valid, new, line, ahead = lax.optimization_barrier((info, valid, new, line, ahead))
    own = [line] + from_all(from_second, lambda _: line)
    ahead = split_ahead(cache, ahead, 1, AHEAD - 1)
    *own, ahead = lax.optimization_barrier((*own, ahead))
    other = [from_twin(part) for part in own]

    sent, mine = attend(info, valid, own, other, ahead, cache, new)
    parts = merge_twins(info, mine, from_twin(sent))
    zs = merge_four([parts[0]] + from_all(from_second, lambda s: parts[SIDE - s]))
    rows = merge_final([zs] + from_all(from_first, lambda _: zs))

    own = [rows] + from_all(from_second, lambda _: rows)
    other = [from_twin(part) for part in own]
    keep, *sends = project(info, own, other, out_weight)
    total = keep
    for d in (1, 2, 3):
        total = total + from_plane(sends[d - 1], SIDE - d).astype(F32)
    return total.astype(BF16)


def solution(mesh):
    placed = (
        P("ctx", "kvh"),
        P(None, "ctx", "kvh", None),
        P(None, None, "kvh", None),
        P(),
        P("kvh", "ctx"),
    )
    return jax.shard_map(
        on_device, mesh=mesh, in_specs=placed, out_specs=P("kvh", "ctx"), check_vma=False
    )
```
